256 devices in a mesh: expert: 32 (over z, y), tensor: 8 (over x, core).
Axes of the slice: x: 4, y: 4, z: 8, core: 2. Of those that a mesh axis runs over, the one named last changes fastest.
Arguments:
- frames: bfloat16 [4096, 1536], P('expert'), may hold values from -6 to 6
- cotangent: bfloat16 [4096, 1536], P('expert'), may hold values from -6 to 6
- segment_ids: int32 [4096], P('expert'), may hold values from 0 to 2, as said below
- kernel: float32 [31, 1536], replicated, may hold values from -1 to 1
- expert_ids: int32 [4096, 2], P('expert'), may hold values from 0 to 31, all different within a row; in each aligned block of 128 rows (0 to 127, 128 to 255, ...) at most 16 rows name the same one
- gates: bfloat16 [4096, 2], P('expert'), may hold values from 0.099609375 to 1
- w_in: bfloat16 [32, 1536, 6144], P('expert', None, 'tensor'), may hold values from -0.15625 to 0.15625
- w_out: bfloat16 [32, 6144, 1536], P('expert', 'tensor'), may hold values from -0.078125 to 0.078125
Outputs:
- frames_grad: bfloat16 [4096, 1536], P('expert')
- kernel_grad: float32 [31, 1536], replicated
- w_in_grad: bfloat16 [32, 1536, 6144], P('expert', None, 'tensor')
- w_out_grad: bfloat16 [32, 6144, 1536], P('expert', 'tensor')
- gate_grad: float32 [4096, 2], P('expert')
The draws below stay inside these ranges and needn't reach their ends.
Inputs may be any that keep to these rules, and one draw needn't show every extreme that they name: `expert_ids`: within the 128 frames of one index of expert, no expert is chosen more than 16 times. `segment_ids`: never falling along the frames; three utterances, the first ending before frame 4096 // 4 and the last starting at frame 3 * 1024 or later.
All inputs are finite; a program needn't handle non-finite values.
Results may differ from the reference program's by a relative error of at most 0.011.
Values may be sent and summed in bfloat16 or wider, within the bound.
A program may use at most 128 MiB of HBM per device.

```python
import math
import jax
import jax.numpy as jnp
import numpy as np
from jax import lax

D = 1536
H = 6144
KW = 31
TOP = 2
F_DEV = 128
FRAMES = 4096
EXPERTS = 32
CAP = 16
N_EXPERT = 32


def draw_segment_ids(key, part):
    key = jax.random.fold_in(key, 7)
    first_key, second_key = jax.random.split(key)
    first_end = jax.random.randint(first_key, (), F_DEV // 2, FRAMES // 4, dtype=jnp.int32)
    second_end = jax.random.randint(second_key, (), 3 * FRAMES // 4, FRAMES - F_DEV // 2, dtype=jnp.int32)
    position = jnp.arange(FRAMES, dtype=jnp.int32)
    return (position >= first_end).astype(jnp.int32) + (position >= second_end).astype(jnp.int32)


def levels(rng, dims, cuts, low, top_value):
    gain, own = 1.0, jax.random.fold_in(rng, 6)
    for dim, parts in cuts:
        draws = jnp.exp(jax.random.uniform(jax.random.fold_in(own, dim), (parts,), jnp.float32, low / len(cuts), top_value / len(cuts)))
        gain = gain * jnp.repeat(draws, dims[dim] // parts).reshape([-1 if axis == dim else 1 for axis in range(len(dims))])
    return gain


def deal_out(stream_key, own, number, rows, count, top, limit, slope):
    ranking = jax.random.permutation(stream_key, count)
    heavy_load, common = load_shares(count, rows * top, limit, slope, True), load_shares(count, rows * top, limit, slope, False)
    places = jnp.arange(count)

    def named(tallies, offset_by):
        used = int((tallies > 0).sum())
        fixed = max(1, used // 4)
        moved = fixed + (places - fixed + offset_by * (used - fixed)) % max(1, count - fixed)
        return jnp.zeros((count,), jnp.int32).at[ranking[jnp.where(places < fixed, places, moved)]].set(jnp.asarray(tallies, jnp.int32))

    tallies = jnp.where(number % 4 == 0, named(heavy_load, number // 4), named(common, number - number // 4 - 1))
    mixed = jax.random.permutation(jax.random.fold_in(own, 3), count)
    giver, taker = mixed[0:count // 2 * 2:2], mixed[1:count // 2 * 2:2]
    margin = jnp.minimum(tallies[giver] - 1, limit - tallies[taker]) // 2
    margin = jnp.where((giver == ranking[0]) | (taker == ranking[0]) | (tallies[taker] == 0), 0, jnp.maximum(margin, 0))
    moved = jax.random.randint(jax.random.fold_in(own, 4), (count // 2,), 0, 1 << 20) % (margin + 1)
    tallies = tallies.at[giver].add(-moved).at[taker].add(moved)
    labels = jnp.searchsorted(jnp.cumsum(tallies), jnp.arange(rows * top), side="right").astype(jnp.int32)
    table = labels.reshape(top, rows).T
    table = table[jax.random.permutation(jax.random.fold_in(own, 1), rows)]
    offset_by = jax.random.randint(jax.random.fold_in(own, 2), (rows, 1), 0, top)
    return jnp.take_along_axis(table, (jnp.arange(top)[None, :] + offset_by) % top, axis=1)


def load_shares(count, total, limit, slope, full):
    loads = [(1 << 20) // math.isqrt(rank ** slope) + 1 for rank in range(1, count + 1)]
    largest = limit if full else min(limit, max(-(-total // count), total * loads[0] // sum(loads)))
    least = 1 if total - largest >= count - 1 else 0
    given, spare = [largest] + [least] * (count - 1), total - largest - least * (count - 1)
    while spare > 0:
        movable = [i for i in range(1, count) if given[i] < largest] or [i for i in range(1, count) if given[i] < limit]
        mass, left = sum([loads[i] for i in movable]), spare
        for i in movable:
            extra = min(limit - given[i], max(1, left * loads[i] // mass), spare)
            given[i] = given[i] + extra
            spare = spare - extra
    return np.array(given)


def noise(key, dims, width, reach, shards=(), kind=jnp.bfloat16):
    entries = jax.random.normal(key, dims, jnp.float32) * width
    if len(shards) > 0:
        entries = levels(key, dims, shards, -0.22, 0.18) * entries
    return jnp.clip(entries, min=-reach, max=reach).astype(kind)


def setup_inputs(seed: int = 0) -> dict:
    arg_keys = jax.random.split(jax.random.key(seed), 9)
    frames = noise(arg_keys[0], (FRAMES, D), 1.0, 6.0, ((0, 32),))
    cotangent = noise(arg_keys[1], (FRAMES, D), 1.0, 6.0, ((0, 32),))
    segment_ids = draw_segment_ids(jax.random.fold_in(arg_keys[8], 71), 0)
    kernel = noise(arg_keys[3], (KW, D), KW ** -0.5, 1.0, (), jnp.float32)
    expert_ids_keys = jax.random.split(jax.random.fold_in(arg_keys[4], 1), FRAMES // F_DEV)
    expert_ids_turns = jax.random.permutation(jax.random.fold_in(arg_keys[4], 3), FRAMES // F_DEV)
    expert_ids = jax.vmap(lambda own, number: deal_out(jax.random.fold_in(arg_keys[4], 2), own, number, F_DEV, EXPERTS, TOP, CAP, 2))(expert_ids_keys, expert_ids_turns).reshape((FRAMES, TOP))
    gates = jnp.clip(jnp.exp(math.log(1.0) - 2.306499 * jax.random.uniform(arg_keys[5], (FRAMES, TOP), jnp.float32) ** levels(arg_keys[5], (FRAMES, TOP), ((0, 32),), -0.2, 0.2)), 0.099609375, 1.0).astype(jnp.bfloat16)
    w_in = noise(arg_keys[6], (EXPERTS, D, H), D ** -0.5, 0.15625, ((0, 32), (2, 8)))
    w_out = noise(arg_keys[7], (EXPERTS, H, D), H ** -0.5, 0.078125, ((0, 32), (1, 8)))
    return dict(frames=frames, cotangent=cotangent, segment_ids=segment_ids, kernel=kernel, expert_ids=expert_ids, gates=gates, w_in=w_in, w_out=w_out)


def shifted(values, offset, fill):
    count = values.shape[0]
    pad = KW // 2
    widths = [(pad, pad)] + [(0, 0)] * (values.ndim - 1)
    padded = jnp.pad(values, widths, constant_values=fill)
    return lax.dynamic_slice_in_dim(padded, pad + offset, count, 0)


def reference(frames, cotangent, segment_ids, kernel, expert_ids, gates, w_in, w_out):
    pad = KW // 2
    inputs = frames.astype(jnp.float32)
    conv = jnp.zeros_like(inputs)
    masks = []
    for j in range(KW):
        near = shifted(segment_ids, j - pad, -1)
        mask = (near == segment_ids).astype(jnp.float32)
        masks.append(mask)
        conv = conv + kernel[j][None, :] * shifted(inputs, j - pad, 0.0) * mask[:, None]
    mixed = (inputs + conv).astype(jnp.bfloat16)
    flat_count = FRAMES * TOP
    chosen = expert_ids.reshape(-1)
    onehot = (chosen[:, None] == jnp.arange(EXPERTS, dtype=jnp.int32)[None, :]).astype(jnp.int32)
    rank = jnp.sum((jnp.cumsum(onehot, axis=0) - onehot) * onehot, axis=1)
    slots = N_EXPERT * CAP
    table = jnp.full((EXPERTS, slots), flat_count, jnp.int32)
    table = table.at[chosen, rank].set(jnp.arange(flat_count, dtype=jnp.int32))
    zero_row = jnp.zeros((1, D), jnp.bfloat16)
    mixed_rows = jnp.concatenate([jnp.repeat(mixed, TOP, axis=0), zero_row], 0)
    grad_rows = jnp.concatenate([jnp.repeat(cotangent, TOP, axis=0), zero_row], 0)
    gate_rows = jnp.concatenate([gates.reshape(-1), jnp.zeros((1,), jnp.bfloat16)], 0)

    def per_expert(items):
        index, first, second = items
        rows_in = mixed_rows[index]
        rows_grad = grad_rows[index]
        weight = gate_rows[index].astype(jnp.float32)[:, None]
        pre = jnp.dot(rows_in, first, preferred_element_type=jnp.float32)
        sig = jax.nn.sigmoid(pre)
        hidden = (pre * sig).astype(jnp.bfloat16)
        scaled = (weight * rows_grad.astype(jnp.float32)).astype(jnp.bfloat16)
        back = jnp.dot(rows_grad, second.T, preferred_element_type=jnp.float32)
        pre_grad = (back * weight * (sig * (1.0 + pre * (1.0 - sig)))).astype(jnp.bfloat16)
        gate_part = jnp.sum(hidden.astype(jnp.float32) * back, axis=1)
        first_grad = jnp.dot(rows_in.T, pre_grad, preferred_element_type=jnp.float32).astype(jnp.bfloat16)
        second_grad = jnp.dot(hidden.T, scaled, preferred_element_type=jnp.float32).astype(jnp.bfloat16)
        input_grad = jnp.dot(pre_grad, first.T, preferred_element_type=jnp.float32)
        return first_grad, second_grad, input_grad, gate_part

    w_in_grad, w_out_grad, input_grads, gate_parts = lax.map(per_expert, (table, w_in, w_out))
    flat_index = table.reshape(-1)
    routed = jnp.zeros((flat_count + 1, D), jnp.float32).at[flat_index].add(input_grads.reshape(-1, D))
    gate_flat = jnp.zeros((flat_count + 1,), jnp.float32).at[flat_index].add(gate_parts.reshape(-1))
    gate_grad = gate_flat[:flat_count].reshape(FRAMES, TOP)
    mixed_grad = cotangent.astype(jnp.float32) + jnp.sum(routed[:flat_count].reshape(FRAMES, TOP, D), axis=1)
    kernel_rows = []
    transposed = jnp.zeros_like(mixed_grad)
    for j in range(KW):
        kernel_rows.append(jnp.sum(mixed_grad * shifted(inputs, j - pad, 0.0) * masks[j][:, None], axis=0))
        near = shifted(segment_ids, pad - j, -1)
        mask = (near == segment_ids).astype(jnp.float32)
        transposed = transposed + kernel[j][None, :] * shifted(mixed_grad, pad - j, 0.0) * mask[:, None]
    kernel_grad = jnp.stack(kernel_rows, 0)
    frames_grad = (mixed_grad + transposed).astype(jnp.bfloat16)
    return frames_grad, kernel_grad, w_in_grad, w_out_grad, gate_grad
```

```python
import jax
import jax.numpy as jnp
from jax import lax
from jax.experimental import pallas as pl
from jax.experimental.pallas import tpu as pltpu
from jax.sharding import PartitionSpec as P

MESH = pl.DeviceIdType.MESH
F32 = jnp.float32
BF16 = jnp.bfloat16
NZ, NY, NX = 8, 4, 4
NE = NZ * NY
F = 128
D = 1536
HS = 768
KW = 31
CAP = 16
SLOTS = NE * CAP
DX = D // NX
NQ = DX // 128
EXT = F + 32


def full_ds(start, size):
    return pl.ds(pl.multiple_of(start, 128), size)


def body(
    frames, cot, seg, kern, ids, gates, w_in, w_out,
    fg_out, kg_out, wig_out, wog_out, gg_out,
    win, wout, wig, wog, rows, sendbuf, src, hs, hr, fx, sx, gsend, grecv, wcol,
    scaled, hidden, pgrad, gacc, gpsend, gpret, ip, sibrecv, cs, r1, s2, r2, fin, ret,
    pmg, pmr, mgx, fgall, kg, krecv, kred, kall, kfull, gg, posr, posc,
    lsem, hsem, asend, arecv, gsem, xsend, ssend, fl, fr, fo, fs, gpsem, sibsem, rsem,
    retsem, pmsem, mhsem, fgsem, ksem, kfsem, ggsem,
):
    e = lax.axis_index("expert")
    t = lax.axis_index("tensor")
    z, y = lax.div(e, NY), lax.rem(e, NY)
    x, c = lax.div(t, 2), lax.rem(t, 2)
    sib = t + 1 - 2 * c
    xr, xl, xo = lax.rem(x + 1, NX), lax.rem(x + 3, NX), lax.rem(x + 2, NX)
    right, left = xr * 2 + c, xl * 2 + c
    xcols = full_ds(x * DX, DX)

    def offset(i):
        p, dy = lax.div(i, NY), lax.rem(i, NY)
        odd = lax.rem(p, 2)
        dz = odd * lax.div(p + 1, 2) + (1 - odd) * lax.rem(NZ - lax.div(p, 2), NZ)
        return dz, dy

    def ahead(i):
        dz, dy = offset(i)
        return lax.rem(z + dz, NZ) * NY + lax.rem(y + dy, NY)

    def behind(i):
        dz, dy = offset(i)
        return lax.rem(z + NZ - dz, NZ) * NY + lax.rem(y + NY - dy, NY)

    def remote(s, d, ss, rs, ee, tt):
        return pltpu.make_async_remote_copy(
            src_ref=s, dst_ref=d, send_sem=ss, recv_sem=rs, device_id=(ee, tt), device_id_type=MESH
        )

    def wait_recv(ref, sem):
        remote(ref, ref, sem, sem, e, sib).wait_recv()

    def wait_send(ref, sem):
        remote(ref, ref, sem, sem, e, sib).wait_send()

    barrier = pltpu.get_barrier_semaphore()

    @pl.loop(1, NE)
    def _(i):
        pl.semaphore_signal(barrier, inc=1, device_id=(ahead(i), t), device_id_type=MESH)

    @pl.loop(1, 2 * NX)
    def _(i):
        pl.semaphore_signal(
            barrier, inc=1, device_id=(e, lax.rem(t + i, 2 * NX)), device_id_type=MESH
        )

    load_in = pltpu.make_async_copy(w_in, win, lsem.at[0])
    load_out = pltpu.make_async_copy(w_out, wout, lsem.at[1])
    load_in.start()
    load_out.start()

    lane = lax.broadcasted_iota(jnp.int32, (F, F), 1)
    sub = lax.broadcasted_iota(jnp.int32, (F, F), 0)
    eye = lane == sub
    idr = [jnp.broadcast_to(ids[k : k + 1, :], (F, F)).astype(F32) for k in range(2)]
    idc = [v.T for v in idr]

    def place(idf, rank):
        idv = idf.astype(jnp.int32)
        dz = (idv // NY - z + NZ) & (NZ - 1)
        dy = (idv - (idv // NY) * NY - y + NY) & (NY - 1)
        p = jnp.maximum(jnp.where(dz <= NZ // 2, 2 * dz - 1, 2 * NZ - 2 * dz), 0)
        return (p * NY + dy) * CAP + rank.astype(jnp.int32)

    for k in range(2):
        hits = jnp.where(idc[0] == idr[k], 1.0, 0.0) + jnp.where(idc[1] == idr[k], 1.0, 0.0)
        rank = jnp.sum(jnp.where(sub < lane, hits, 0.0), axis=0, keepdims=True)
        posr[k] = place(idr[k], jnp.broadcast_to(rank, (F, F)))
        hits = jnp.where(idr[0] == idc[k], 1.0, 0.0) + jnp.where(idr[1] == idc[k], 1.0, 0.0)
        rank = jnp.sum(jnp.where(lane < sub, hits, 0.0), axis=1, keepdims=True)
        posc[k] = place(idc[k], jnp.broadcast_to(rank, (F, F)))

    for g in range(4):
        total = jnp.zeros((1, F), F32)
        for k in range(2):
            gcol = jnp.broadcast_to(gates[k : k + 1, :].astype(F32), (F, F)).T
            total += jnp.sum(
                jnp.where(posc[k] == lane + g * F, gcol, 0.0), axis=0, keepdims=True
            )
        gsend[g] = total
    grecv[0] = gsend[0]

    segr = jnp.broadcast_to(seg[...], (F, F)).astype(F32)
    segc = segr.T
    sx[16 : 16 + F, :] = segc
    hs[0, :, 0:DX] = frames[0:16, xcols]
    hs[1, :, 0:DX] = frames[F - 16 : F, xcols]
    hs[0, :, DX : DX + 128] = segc[0:16].astype(BF16)
    hs[1, :, DX : DX + 128] = segc[F - 16 : F].astype(BF16)

    @pl.loop(0, NQ)
    def _(q):
        fx[16 : 16 + F, full_ds(q * 128, 128)] = frames[:, full_ds(x * DX + q * 128, 128)].astype(
            F32
        )

    pl.semaphore_wait(barrier, NE - 1 + 2 * NX - 1)

    before, after = lax.rem(e + NE - 1, NE), lax.rem(e + 1, NE)
    halo_up = remote(hs.at[1], hr.at[0], hsem.at[0], hsem.at[1], after, t)
    halo_down = remote(hs.at[0], hr.at[1], hsem.at[2], hsem.at[3], before, t)
    halo_up.start()
    halo_down.start()

    def take_halo():
        halo_up.wait_recv()
        halo_down.wait_recv()
        for q in range(NQ):
            fx[0:16, 128 * q : 128 * q + 128] = hr[0, :, 128 * q : 128 * q + 128].astype(F32)
            fx[16 + F : EXT, 128 * q : 128 * q + 128] = hr[1, :, 128 * q : 128 * q + 128].astype(
                F32
            )
        sx[0:16, :] = jnp.where(e == 0, -1.0, hr[0, :, DX : DX + 128].astype(F32))
        sx[16 + F : EXT, :] = jnp.where(e == NE - 1, -1.0, hr[1, :, DX : DX + 128].astype(F32))

    def conv(ext, q, backwards):
        cols = full_ds(q * 128, 128)
        kcols = full_ds(x * DX + q * 128, 128)
        acc = jnp.zeros((F, 128), F32)
        own = sx[16 : 16 + F, :]
        for j in range(KW):
            tap = kern[KW - 1 - j if backwards else j, kcols].reshape(1, 128)
            acc += jnp.where(sx[j + 1 : j + 1 + F, :] == own, ext[j + 1 : j + 1 + F, cols] * tap, 0.0)
        return acc + ext[16 : 16 + F, cols]

    @pl.when(c == 0)
    def _():
        take_halo()

        @pl.loop(0, NQ)
        def _(q):
            src[:, full_ds(q * 128, 128)] = conv(fx, q, False).astype(BF16)

    @pl.when(c == 1)
    def _():
        src[...] = cot[:, xcols]

    @pl.loop(0, 4)
    def _(g):
        slot = sub + g * F
        onehot = jnp.where((posr[0] == slot) | (posr[1] == slot), 1.0, 0.0).astype(BF16)
        gr = full_ds(g * F, F)
        sendbuf[gr, :] = jnp.dot(onehot, src[...], preferred_element_type=F32).astype(BF16)

        @pl.loop(0, 8)
        def _(q):
            i = g * 8 + q
            blk = pl.ds(pl.multiple_of(i * CAP, CAP), CAP)

            @pl.when(i > 0)
            def _():
                to = ahead(i)
                remote(
                    sendbuf.at[blk, :], rows.at[c, blk, xcols], asend.at[0], arecv.at[g], to, t
                ).start()
                remote(gsend.at[g], grecv.at[i], asend.at[1], gsem.at[0], to, t).start()

    rows[c, 0:CAP, xcols] = sendbuf[0:CAP, :]

    @pl.when(c == 1)
    def _():
        take_halo()

    def region(g, xs):
        return rows.at[c, g * F : g * F + F, full_ds(xs * DX, DX)]

    def to_sibling(g, xs):
        r = region(g, xs)
        remote(r, r, ssend.at[0], fs.at[g], e, sib).start()

    def spread(g):
        if g == 0:
            wait_recv(rows.at[c, CAP:F, xcols], arecv.at[0])
        else:
            wait_recv(region(g, x), arecv.at[g])
        r = region(g, x)
        remote(r, r, xsend.at[0], fl.at[g], e, right).start()
        remote(r, r, xsend.at[1], fr.at[g], e, left).start()
        to_sibling(g, x)

    def relay(g):
        r = region(g, xl)
        wait_recv(r, fl.at[g])
        if g % 2 == 0:
            remote(r, r, xsend.at[2], fo.at[g], e, right).start()
        to_sibling(g, xl)
        r = region(g, xr)
        wait_recv(r, fr.at[g])
        if g % 2 == 1:
            remote(r, r, xsend.at[2], fo.at[g], e, left).start()
        to_sibling(g, xr)

    def opposite(g):
        wait_recv(region(g, xo), fo.at[g])
        to_sibling(g, xo)

    def from_sibling(g):
        wait_recv(rows.at[1 - c, g * F : g * F + F, :], fs.at[g])

    def weigh(g):
        parts = [jnp.broadcast_to(grecv[8 * g + q], (CAP, F)) for q in range(8)]
        w = jnp.sum(jnp.where(eye, jnp.concatenate(parts, axis=0), 0.0), axis=1, keepdims=True)
        wcol[g * F : g * F + F, :] = jnp.broadcast_to(w, (F, 128))

    def work(h):
        hr_ = slice(256 * h, 256 * h + 256)
        gacc[hr_, :] = jnp.zeros((256, 128), F32)

        @pl.loop(0, HS // 256)
        def _(n):
            cols = full_ds(n * 256, 256)
            pre = jnp.dot(rows[0, hr_, :], win[:, cols], preferred_element_type=F32)
            back = lax.dot_general(
                rows[1, hr_, :], wout[cols, :], (((1,), (1,)), ((), ())), preferred_element_type=F32
            )
            sig = jax.nn.sigmoid(pre)
            hid = (pre * sig).astype(BF16)
            hidden[hr_, cols] = hid
            prod = hid.astype(F32) * back
            gacc[hr_, :] += prod[:, 0:128] + prod[:, 128:256]
            w = wcol[hr_, 0:1]
            pgrad[hr_, cols] = (back * w * (sig * (1.0 + pre * (1.0 - sig)))).astype(BF16)

        for g in (2 * h, 2 * h + 1):
            part = jnp.sum(gacc[g * F : g * F + F, :], axis=1, keepdims=True)
            row = jnp.sum(
                jnp.where(eye, jnp.broadcast_to(part, (F, F)), 0.0), axis=0, keepdims=True
            )
            gpsend[g] = row
            if g == 0:
                gpret[0] = row

        @pl.loop(max(16 * h, 1), 16 * h + 16)
        def _(i):
            g = lax.div(i, 8)
            remote(gpsend.at[g], gpret.at[i], gpsem.at[0], gpsem.at[1], behind(i), t).start()

    def scale(h):
        @pl.loop(0, D // 256)
        def _(n):
            cols = full_ds(n * 256, 256)
            rh = slice(256 * h, 256 * h + 256)
            scaled[rh, cols] = (wcol[rh, 0:1] * rows[1, rh, cols].astype(F32)).astype(BF16)

    def inputs_grad(h):
        rh = slice(256 * h, 256 * h + 256)

        @pl.loop(0, 3)
        def _(n):
            cols = full_ds(n * 512, 512)
            ip[rh, cols] = lax.dot_general(
                pgrad[rh, :], win[cols, :], (((1,), (1,)), ((), ())), preferred_element_type=F32
            ).astype(BF16)

        other = full_ds((2 * h + 1 - c) * F, F)
        remote(ip.at[other, :], sibrecv.at[h], sibsem.at[0], sibsem.at[1 + h], e, sib).start()

    def ring1(h):
        wait_recv(sibrecv.at[h], sibsem.at[1 + h])
        own = full_ds((2 * h + c) * F, F)
        cs[h] = (ip[own, :].astype(F32) + sibrecv[h].astype(F32)).astype(BF16)
        oc = full_ds(xo * DX, DX)
        remote(cs.at[h, 0:64, oc], r1.at[h, 0], rsem.at[0], rsem.at[2 + h], e, right).start()
        remote(cs.at[h, 64:128, oc], r1.at[h, 1], rsem.at[1], rsem.at[4 + h], e, left).start()

    def ring2(h):
        wait_recv(r1.at[h, 0], rsem.at[2 + h])
        rc = full_ds(xr * DX, DX)
        s2[h, 0, 0:64, :] = (cs[h, 0:64, rc].astype(F32) + r1[h, 0].astype(F32)).astype(BF16)
        s2[h, 0, 64:128, :] = cs[h, 64:128, rc]
        remote(s2.at[h, 0], r2.at[h, 0], rsem.at[6], rsem.at[8 + h], e, right).start()
        wait_recv(r1.at[h, 1], rsem.at[4 + h])
        lc = full_ds(xl * DX, DX)
        s2[h, 1, 64:128, :] = (cs[h, 64:128, lc].astype(F32) + r1[h, 1].astype(F32)).astype(BF16)
        s2[h, 1, 0:64, :] = cs[h, 0:64, lc]
        remote(s2.at[h, 1], r2.at[h, 1], rsem.at[7], rsem.at[10 + h], e, left).start()

    def ring3(h):
        wait_recv(r2.at[h, 0], rsem.at[8 + h])
        wait_recv(r2.at[h, 1], rsem.at[10 + h])
        fin[h] = (
            cs[h, :, xcols].astype(F32) + r2[h, 0].astype(F32) + r2[h, 1].astype(F32)
        ).astype(BF16)

        @pl.loop(0, 8)
        def _(q):
            i = (2 * h + c) * 8 + q
            blk = pl.ds(pl.multiple_of(q * CAP, CAP), CAP)

            @pl.when(i > 0)
            def _():
                remote(
                    fin.at[h, blk, :], ret.at[h, blk, :], retsem.at[0], retsem.at[1 + h], behind(i), t
                ).start()

        if h == 0:

            @pl.when(c == 0)
            def _():
                ret[0, 0:CAP, :] = fin[0, 0:CAP, :]

    def first_grad(lo, hi):
        @pl.loop(lo, hi)
        def _(m):
            cols = full_ds(m * 256, 256)
            wig[cols, :] = lax.dot_general(
                rows[0, :, cols], pgrad[...], (((0,), (0,)), ((), ())), preferred_element_type=F32
            ).astype(BF16)

    def second_grad(lo, hi):
        @pl.loop(lo, hi)
        def _(m):
            cols = full_ds(m * 256, 256)
            for n in range(2):
                nc = slice(n * 768, n * 768 + 768)
                wog[cols, nc] = lax.dot_general(
                    hidden[:, cols], scaled[:, nc], (((0,), (0,)), ((), ())),
                    preferred_element_type=F32,
                ).astype(BF16)

    spread(0)
    spread(1)
    relay(0)
    spread(2)
    relay(1)
    opposite(0)
    spread(3)
    relay(2)
    opposite(1)
    wait_recv(grecv.at[1:NE], gsem.at[0])
    for g in range(4):
        weigh(g)
    load_in.wait()
    load_out.wait()
    from_sibling(0)
    from_sibling(1)
    work(0)
    relay(3)
    opposite(2)
    inputs_grad(0)
    opposite(3)
    scale(0)
    ring1(0)
    from_sibling(2)
    from_sibling(3)
    work(1)
    ring2(0)
    inputs_grad(1)
    ring3(0)
    scale(1)
    first_grad(0, 2)
    ring1(1)
    first_grad(2, 6)
    ring2(1)
    store_in = pltpu.make_async_copy(wig, wig_out, lsem.at[2])
    store_in.start()
    second_grad(0, 2)
    ring3(1)
    second_grad(2, 3)
    store_out = pltpu.make_async_copy(wog, wog_out, lsem.at[3])
    store_out.start()

    wait_recv(gpret.at[1:NE], gpsem.at[1])
    gcols = [jnp.zeros((F, F), F32) for _ in range(2)]
    for g in range(4):
        row = jnp.zeros((1, F), F32)
        for q in range(8):
            row += jnp.where(lax.div(lane[0:1, :], CAP) == q, gpret[8 * g + q], 0.0)
        row = jnp.broadcast_to(row, (F, F))
        for k in range(2):
            gcols[k] += jnp.where(posc[k] == lane + g * F, row, 0.0)
    for k in range(2):
        col = jnp.sum(gcols[k], axis=1, keepdims=True)
        gg[t, k : k + 1, :] = jnp.sum(
            jnp.where(eye, jnp.broadcast_to(col, (F, F)), 0.0), axis=0, keepdims=True
        )

    @pl.loop(1, 2 * NX)
    def _(i):
        remote(
            gg.at[t], gg.at[t], ggsem.at[0], ggsem.at[1], e, lax.rem(t + i, 2 * NX)
        ).start()

    @pl.when(c == 0)
    def _():
        wait_recv(ret.at[0, CAP:F, :], retsem.at[1])

    @pl.when(c == 1)
    def _():
        wait_recv(ret.at[0], retsem.at[1])

    wait_recv(ret.at[1], retsem.at[2])
    picks = []
    for h in range(2):
        slot = lane + (2 * h + c) * F
        picks.append(
            jnp.where((posc[0] == slot) | (posc[1] == slot), 1.0, 0.0).astype(BF16)
        )
    pmg[...] = jnp.dot(picks[0], ret[0], preferred_element_type=F32) + jnp.dot(
        picks[1], ret[1], preferred_element_type=F32
    )
    swap = remote(pmg, pmr, pmsem.at[0], pmsem.at[1], e, sib)
    swap.start()
    swap.wait_recv()
    mgx[16 : 16 + F, :] = cot[:, xcols].astype(F32) + (pmg[...] + pmr[...])

    @pl.when(c == 0)
    def _():
        up = remote(
            mgx.at[F : F + 16, :], mgx.at[0:16, :], mhsem.at[0], mhsem.at[1], after, t
        )
        down = remote(
            mgx.at[16:32, :], mgx.at[16 + F : EXT, :], mhsem.at[2], mhsem.at[3], before, t
        )
        up.start()
        down.start()
        up.wait_recv()
        down.wait_recv()

        @pl.loop(0, NQ)
        def _(q):
            fgall[:, full_ds(x * DX + q * 128, 128)] = conv(mgx, q, True).astype(BF16)

        @pl.loop(1, 2 * NX)
        def _(i):
            r = fgall.at[:, xcols]
            remote(r, r, fgsem.at[0], fgsem.at[1], e, lax.rem(t + i, 2 * NX)).start()

        wait_recv(fgall.at[:, 0 : 3 * DX], fgsem.at[1])
        wait_recv(kfull, kfsem.at[1])
        wait_send(ip.at[0 : 3 * F, 0:896], fgsem.at[0])
        up.wait_send()
        down.wait_send()

    @pl.when(c == 1)
    def _():
        kg[...] = jnp.zeros_like(kg)

        @pl.loop(0, NQ)
        def _(q):
            cols = full_ds(q * 128, 128)
            own = sx[16 : 16 + F, :]
            mg = mgx[16 : 16 + F, cols]
            for j in range(KW):
                prod = jnp.where(
                    sx[j + 1 : j + 1 + F, :] == own, fx[j + 1 : j + 1 + F, cols] * mg, 0.0
                )
                kg[j, pl.ds(q, 1), :] = jnp.sum(prod, axis=0, keepdims=True)

        krecv[0] = kg[e]

        @pl.loop(1, NE)
        def _(i):
            to = ahead(i)
            remote(kg.at[to], krecv.at[i], ksem.at[0], ksem.at[1], to, t).start()

        wait_recv(krecv.at[1:NE], ksem.at[1])
        kred[...] = jnp.sum(krecv[...], axis=0)
        kall[0] = kred[...]
        korder = kall

        @pl.loop(1, NE)
        def _(i):
            remote(kred, korder.at[i], ksem.at[2], ksem.at[3], ahead(i), t).start()

        wait_recv(kall.at[1:NE], ksem.at[3])

        @pl.loop(0, NE)
        def _(i):
            kfull[x, behind(i)] = kall[i]

        @pl.loop(1, 2 * NX)
        def _(i):
            remote(
                kfull.at[x], kfull.at[x], kfsem.at[0], kfsem.at[1], e, lax.rem(t + i, 2 * NX)
            ).start()

        wait_recv(kfull.at[0:3], kfsem.at[1])
        wait_recv(fgall, fgsem.at[1])
        wait_send(kg.at[1:NE], ksem.at[0])
        wait_send(kg.at[1:NE], ksem.at[2])
        wait_send(ip.at[0 : 2 * F, 0:896], kfsem.at[0])

    wait_recv(gg.at[1 : 2 * NX], ggsem.at[1])
    gg_out[...] = jnp.sum(gg[...], axis=0)
    fg_out[...] = fgall[...]
    for xs in range(NX):
        for q in range(NQ):
            kg_out[:, xs * DX + q * 128 : xs * DX + q * 128 + 128] = kfull[xs, 0:KW, q, :]

    store_in.wait()
    store_out.wait()
    halo_up.wait_send()
    halo_down.wait_send()
    wait_send(sendbuf.at[CAP:SLOTS, :], asend.at[0])
    wait_send(grecv.at[1:NE], asend.at[1])
    wait_send(rows.at[c, :, xcols], xsend.at[0])
    wait_send(rows.at[c, :, xcols], xsend.at[1])
    wait_send(rows.at[c, :, xcols], xsend.at[2])
    wait_send(rows.at[c], ssend.at[0])
    wait_send(gpret.at[1:NE], gpsem.at[0])
    wait_send(sibrecv, sibsem.at[0])
    wait_send(r1.at[:, 0], rsem.at[0])
    wait_send(r1.at[:, 1], rsem.at[1])
    wait_send(s2.at[:, 0], rsem.at[6])
    wait_send(s2.at[:, 1], rsem.at[7])

    @pl.when(c == 0)
    def _():
        wait_send(ip.at[CAP : 2 * F, 0:DX], retsem.at[0])

    @pl.when(c == 1)
    def _():
        wait_send(ip.at[0 : 2 * F, 0:DX], retsem.at[0])

    swap.wait_send()
    wait_send(gg.at[1 : 2 * NX], ggsem.at[0])


def on_device(frames, cotangent, segment_ids, kernel, expert_ids, gates, w_in, w_out):
    vmem = pl.BlockSpec(memory_space=pltpu.VMEM)
    anywhere = pl.BlockSpec(memory_space=pl.ANY)
    dma = pltpu.SemaphoreType.DMA
    V = pltpu.VMEM
    scratch = dict(
        win=V((D, HS), BF16),
        wout=V((HS, D), BF16),
        wig=V((D, HS), BF16),
        wog=V((HS, D), BF16),
        rows=V((2, SLOTS, D), BF16),
        sendbuf=V((SLOTS, DX), BF16),
        src=V((F, DX), BF16),
        hs=V((2, 16, DX + 128), BF16),
        hr=V((2, 16, DX + 128), BF16),
        fx=V((EXT, DX), F32),
        sx=V((EXT, 128), F32),
        gsend=V((4, 1, 128), F32),
        grecv=V((NE, 1, 128), F32),
        wcol=V((SLOTS, 128), F32),
        scaled=V((SLOTS, D), BF16),
        hidden=V((SLOTS, HS), BF16),
        pgrad=V((SLOTS, HS), BF16),
        gacc=V((SLOTS, 128), F32),
        gpsend=V((4, 1, 128), F32),
        gpret=V((NE, 1, 128), F32),
        ip=V((SLOTS, D), BF16),
        sibrecv=V((2, F, D), BF16),
        cs=V((2, F, D), BF16),
        r1=V((2, 2, F // 2, DX), BF16),
        s2=V((2, 2, F, DX), BF16),
        r2=V((2, 2, F, DX), BF16),
        fin=V((2, F, DX), BF16),
        ret=V((2, F, DX), BF16),
        pmg=V((F, DX), F32),
        pmr=V((F, DX), F32),
        mgx=V((EXT, DX), F32),
        fgall=V((F, D), BF16),
        kg=V((NE, 4, 128), F32),
        krecv=V((NE, 4, 128), F32),
        kred=V((4, 128), F32),
        kall=V((NE, 4, 128), F32),
        kfull=V((NX, NE, 4, 128), F32),
        gg=V((2 * NX, 2, 128), F32),
        posr=V((2, F, F), jnp.int32),
        posc=V((2, F, F), jnp.int32),
        lsem=dma((4,)),
        hsem=dma((4,)),
        asend=dma((2,)),
        arecv=dma((4,)),
        gsem=dma((1,)),
        xsend=dma((3,)),
        ssend=dma((1,)),
        fl=dma((4,)),
        fr=dma((4,)),
        fo=dma((4,)),
        fs=dma((4,)),
        gpsem=dma((2,)),
        sibsem=dma((3,)),
        rsem=dma((12,)),
        retsem=dma((3,)),
        pmsem=dma((2,)),
        mhsem=dma((4,)),
        fgsem=dma((2,)),
        ksem=dma((4,)),
        kfsem=dma((2,)),
        ggsem=dma((2,)),
    )
    fg, kg, wig, wog, gg = pl.pallas_call(
        body,
        out_shape=(
            jax.ShapeDtypeStruct((F, D), BF16),
            jax.ShapeDtypeStruct((KW, D), F32),
            jax.ShapeDtypeStruct((D, HS), BF16),
            jax.ShapeDtypeStruct((HS, D), BF16),
            jax.ShapeDtypeStruct((2, F), F32),
        ),
        in_specs=[vmem] * 6 + [anywhere] * 2,
        out_specs=(vmem, vmem, anywhere, anywhere, vmem),
        scratch_shapes=list(scratch.values()),
        compiler_params=pltpu.CompilerParams(
            collective_id=0, has_side_effects=True, vmem_limit_bytes=56 * 1024 * 1024
        ),
    )(
        frames,
        cotangent,
        segment_ids.reshape(1, F),
        kernel,
        expert_ids.T,
        gates.T,
        w_in[0],
        w_out[0],
    )
    return fg, kg, wig[None], wog[None], gg.T


def solution(mesh):
    return jax.shard_map(
        on_device,
        mesh=mesh,
        in_specs=(
            P("expert", None),
            P("expert", None),
            P("expert"),
            P(),
            P("expert", None),
            P("expert", None),
            P("expert", None, "tensor"),
            P("expert", "tensor", None),
        ),
        out_specs=(
            P("expert", None),
            P(),
            P("expert", None, "tensor"),
            P("expert", "tensor", None),
            P("expert", None),
        ),
        check_vma=False,
    )
```

```python
import jax
import jax.numpy as jnp
from jax import lax
from jax.experimental import pallas as pl
from jax.experimental.pallas import tpu as pltpu
from jax.sharding import PartitionSpec as P

MESH = pl.DeviceIdType.MESH
F32 = jnp.float32
BF16 = jnp.bfloat16
NZ, NY, NX = 8, 4, 4
NE = NZ * NY
F = 128
D = 1536
HS = 768
KW = 31
CAP = 16
SLOTS = NE * CAP
DX = D // NX
NQ = DX // 128
EXT = F + 32


def full_ds(start, size):
    return pl.ds(pl.multiple_of(start, 128), size)


def body(
    frames_in, cot_in, seg_in, kern_in, ids_in, gates_in, w_in, w_out,
    fg_out, kg_out, wig, wog, gg_out,
    frames, cot, seg, kern, ids, gates,
    win, wout, rows, sendbuf, src, hs, hr, fx, sx, gsend, grecv, wcol,
    scaled, hidden, pgrad, gacc, gpsend, gpx, gprow, gpret, ip, sibrecv, cs, r1, s2, r2, fin, ret,
    pmg, pmr, mgx, fgall, kg, krecv, kred, kfull, gg, posr, posc,
    lsem, hsem, asend, arecv, gsem, xsend, ssend, fl, fr, fo, fs, gpsem, sibsem, rsem,
    retsem, pmsem, mhsem, fgsem, ksem, kfsem, ggsem,
):
    e = lax.axis_index("expert")
    t = lax.axis_index("tensor")
    z, y = lax.div(e, NY), lax.rem(e, NY)
    x, c = lax.div(t, 2), lax.rem(t, 2)
    sib = t + 1 - 2 * c
    xr, xl, xo = lax.rem(x + 1, NX), lax.rem(x + 3, NX), lax.rem(x + 2, NX)
    right, left, facing = xr * 2 + c, xl * 2 + c, xo * 2 + c
    xcols = full_ds(x * DX, DX)

    zt = [lax.rem(z + k, NZ) * NY for k in range(NZ)]
    yt = [lax.rem(y + k, NY) for k in range(NY)]

    def offset(i):
        p = i // NY
        return ((p + 1) // 2 if p % 2 else (NZ - p // 2) % NZ), i % NY

    def ahead(i):
        dz, dy = offset(i)
        return zt[dz] + yt[dy]

    def behind(i):
        dz, dy = offset(i)
        return zt[(NZ - dz) % NZ] + yt[(NY - dy) % NY]

    def remote(s, d, ss, rs, ee, tt):
        return pltpu.make_async_remote_copy(
            src_ref=s, dst_ref=d, send_sem=ss, recv_sem=rs, device_id=(ee, tt), device_id_type=MESH
        )

    def wait_recv(ref, sem):
        remote(ref, ref, sem, sem, e, sib).wait_recv()

    def wait_send(ref, sem):
        remote(ref, ref, sem, sem, e, sib).wait_send()

    barrier = pltpu.get_barrier_semaphore()

    for i in range(1, NE):
        pl.semaphore_signal(barrier, inc=1, device_id=(ahead(i), t), device_id_type=MESH)
    for i in range(1, 2 * NX):
        pl.semaphore_signal(
            barrier, inc=1, device_id=(e, lax.rem(t + i, 2 * NX)), device_id_type=MESH
        )
    pairs = (
        (ids_in, ids), (gates_in, gates), (seg_in, seg), (frames_in, frames), (cot_in, cot),
        (kern_in, kern), (w_in, win), (w_out, wout),
    )
    loads = [pltpu.make_async_copy(a, b, lsem.at[k]) for k, (a, b) in enumerate(pairs)]
    for load in loads:
        load.start()
    for load in loads[:3]:
        load.wait()

    lane = lax.broadcasted_iota(jnp.int32, (F, F), 1)
    sub = lax.broadcasted_iota(jnp.int32, (F, F), 0)
    eye = lane == sub
    idr = [jnp.broadcast_to(ids[k : k + 1, :], (F, F)).astype(F32) for k in range(2)]
    idc = [v.T for v in idr]

    def place(idf, rank):
        idv = idf.astype(jnp.int32)
        dz = (idv // NY - z + NZ) & (NZ - 1)
        dy = (idv - (idv // NY) * NY - y + NY) & (NY - 1)
        p = jnp.maximum(jnp.where(dz <= NZ // 2, 2 * dz - 1, 2 * NZ - 2 * dz), 0)
        return (p * NY + dy) * CAP + rank.astype(jnp.int32)

    for k in range(2):
        hits = jnp.where(idc[0] == idr[k], 1.0, 0.0) + jnp.where(idc[1] == idr[k], 1.0, 0.0)
        rank = jnp.sum(jnp.where(sub < lane, hits, 0.0), axis=0, keepdims=True)
        posr[k] = place(idr[k], jnp.broadcast_to(rank, (F, F)))
        hits = jnp.where(idr[0] == idc[k], 1.0, 0.0) + jnp.where(idr[1] == idc[k], 1.0, 0.0)
        rank = jnp.sum(jnp.where(lane < sub, hits, 0.0), axis=1, keepdims=True)
        posc[k] = place(idc[k], jnp.broadcast_to(rank, (F, F)))

    for g in range(4):
        total = jnp.zeros((1, F), F32)
        for k in range(2):
            gcol = jnp.broadcast_to(gates[k : k + 1, :].astype(F32), (F, F)).T
            total += jnp.sum(
                jnp.where(posc[k] == lane + g * F, gcol, 0.0), axis=0, keepdims=True
            )
        gsend[g] = total

    @pl.when(c == 1)
    def _():
        grecv[0] = gsend[0]

    for load in loads[3:6]:
        load.wait()
    segr = jnp.broadcast_to(seg[...], (F, F)).astype(F32)
    segc = segr.T
    sx[16 : 16 + F, :] = segc
    hs[0, :, 0:DX] = frames[0:16, xcols]
    hs[1, :, 0:DX] = frames[F - 16 : F, xcols]
    hs[0, :, DX : DX + 128] = segc[0:16].astype(BF16)
    hs[1, :, DX : DX + 128] = segc[F - 16 : F].astype(BF16)

    @pl.loop(0, NQ)
    def _(q):
        fx[16 : 16 + F, full_ds(q * 128, 128)] = frames[:, full_ds(x * DX + q * 128, 128)].astype(
            F32
        )

    pl.semaphore_wait(barrier, NE - 1 + 2 * NX - 1)

    before, after = lax.rem(e + NE - 1, NE), lax.rem(e + 1, NE)
    halo_up = remote(hs.at[1], hr.at[0], hsem.at[0], hsem.at[1], after, t)
    halo_down = remote(hs.at[0], hr.at[1], hsem.at[2], hsem.at[3], before, t)
    halo_up.start()
    halo_down.start()

    def take_halo():
        halo_up.wait_recv()
        halo_down.wait_recv()
        for q in range(NQ):
            fx[0:16, 128 * q : 128 * q + 128] = hr[0, :, 128 * q : 128 * q + 128].astype(F32)
            fx[16 + F : EXT, 128 * q : 128 * q + 128] = hr[1, :, 128 * q : 128 * q + 128].astype(
                F32
            )
        sx[0:16, :] = jnp.where(e == 0, -1.0, hr[0, :, DX : DX + 128].astype(F32))
        sx[16 + F : EXT, :] = jnp.where(e == NE - 1, -1.0, hr[1, :, DX : DX + 128].astype(F32))

    def conv(ext, q, backwards):
        cols = full_ds(q * 128, 128)
        kcols = full_ds(x * DX + q * 128, 128)
        acc = jnp.zeros((F, 128), F32)
        own = sx[16 : 16 + F, :]
        for j in range(KW):
            tap = kern[KW - 1 - j if backwards else j, kcols].reshape(1, 128)
            acc += jnp.where(sx[j + 1 : j + 1 + F, :] == own, ext[j + 1 : j + 1 + F, cols] * tap, 0.0)
        return acc + ext[16 : 16 + F, cols]

    @pl.when(c == 0)
    def _():
        take_halo()

        @pl.loop(0, NQ)
        def _(q):
            src[:, full_ds(q * 128, 128)] = conv(fx, q, False).astype(BF16)

    @pl.when(c == 1)
    def _():
        src[...] = cot[:, xcols]

    def issue(g):
        slot = sub + g * F
        onehot = jnp.where((posr[0] == slot) | (posr[1] == slot), 1.0, 0.0).astype(BF16)
        gr = slice(g * F, g * F + F)
        sendbuf[gr, :] = jnp.dot(onehot, src[...], preferred_element_type=F32).astype(BF16)
        for i in range(max(8 * g, 1), 8 * g + 8):
            blk = slice(i * CAP, i * CAP + CAP)
            remote(
                sendbuf.at[blk, :], rows.at[c, blk, xcols], asend.at[0], arecv.at[g], ahead(i), t
            ).start()
        if g == 0:
            rows[c, 0:CAP, xcols] = sendbuf[0:CAP, :]

    issue(0)
    issue(1)

    @pl.when(c == 1)
    def _():
        for i in range(1, NE):
            remote(
                gsend.at[i // 8], grecv.at[i], asend.at[1], gsem.at[0], ahead(i), t
            ).start()

    @pl.when(c == 1)
    def _():
        take_halo()

    def region(g, xs):
        return rows.at[c, g * F : g * F + F, full_ds(xs * DX, DX)]

    def to_sibling(g, xs):
        r = region(g, xs)
        remote(r, r, ssend.at[0], fs.at[g], e, sib).start()

    def spread(g):
        if g == 0:
            wait_recv(rows.at[c, CAP:F, xcols], arecv.at[0])
        else:
            wait_recv(region(g, x), arecv.at[g])
        r = region(g, x)
        remote(r, r, xsend.at[0], fl.at[g], e, right).start()
        remote(r, r, xsend.at[1], fr.at[g], e, left).start()
        to_sibling(g, x)

    def relay(g):
        r = region(g, xl)
        wait_recv(r, fl.at[g])
        lo = rows.at[c, g * F : g * F + F // 2, full_ds(xl * DX, DX)]
        remote(lo, lo, xsend.at[2], fo.at[g], e, right).start()
        to_sibling(g, xl)
        r = region(g, xr)
        wait_recv(r, fr.at[g])
        hi = rows.at[c, g * F + F // 2 : g * F + F, full_ds(xr * DX, DX)]
        remote(hi, hi, xsend.at[2], fo.at[g], e, left).start()
        to_sibling(g, xr)

    def opposite(g):
        wait_recv(region(g, xo), fo.at[g])
        to_sibling(g, xo)

    def from_sibling(g):
        wait_recv(rows.at[1 - c, g * F : g * F + F, :], fs.at[g])

    def weigh(g):
        parts = [jnp.broadcast_to(grecv[8 * g + q], (CAP, F)) for q in range(8)]
        w = jnp.sum(jnp.where(eye, jnp.concatenate(parts, axis=0), 0.0), axis=1, keepdims=True)
        wcol[g * F : g * F + F, :] = jnp.broadcast_to(w, (F, 128))

    def work(h):
        hr_ = slice(256 * h, 256 * h + 256)
        gacc[hr_, :] = jnp.zeros((256, 128), F32)

        @pl.loop(0, HS // 256)
        def _(n):
            cols = full_ds(n * 256, 256)
            pre = jnp.dot(rows[0, hr_, :], win[:, cols], preferred_element_type=F32)
            back = lax.dot_general(
                rows[1, hr_, :], wout[cols, :], (((1,), (1,)), ((), ())), preferred_element_type=F32
            )
            sig = jax.nn.sigmoid(pre)
            hid = (pre * sig).astype(BF16)
            hidden[hr_, cols] = hid
            prod = hid.astype(F32) * back
            gacc[hr_, :] += prod[:, 0:128] + prod[:, 128:256]
            w = wcol[hr_, 0:1]
            pgrad[hr_, cols] = (back * w * (sig * (1.0 + pre * (1.0 - sig)))).astype(BF16)

        for g in (2 * h, 2 * h + 1):
            part = jnp.sum(gacc[g * F : g * F + F, :], axis=1, keepdims=True)
            row = jnp.sum(
                jnp.where(eye, jnp.broadcast_to(part, (F, F)), 0.0), axis=0, keepdims=True
            )
            gpsend[g] = row

        for tt in range(4 * h, 4 * h + 4):

            @pl.when(t == tt)
            def _():
                gpx[tt] = gpsend[tt // 2]

            @pl.when(t != tt)
            def _():
                remote(
                    gpsend.at[tt // 2], gpx.at[t], gpsem.at[0], gpsem.at[1], e, tt
                ).start()

    def gates_on():
        wait_recv(gpx.at[1 : 2 * NX], gpsem.at[1])
        gprow[0] = jnp.sum(gpx[...], axis=0)
        dz = c * (x + 1) + (1 - c) * lax.rem(NZ - x, NZ)
        zz = lax.rem(z + NZ - dz, NZ) * NY

        @pl.when(t == 0)
        def _():
            gpret[0] = gprow[0]

        @pl.when(t > 0)
        def _():
            remote(gprow.at[0], gpret.at[0], gpsem.at[2], gpsem.at[3], zz + yt[0], t).start()

        for j in range(1, NY):
            remote(
                gprow.at[0], gpret.at[j], gpsem.at[2], gpsem.at[3], zz + yt[NY - j], t
            ).start()

    def gates_home():
        @pl.when(t == 0)
        def _():
            wait_recv(gpret.at[1:NY], gpsem.at[3])

        @pl.when(t > 0)
        def _():
            wait_recv(gpret, gpsem.at[3])

        row = jnp.zeros((1, F), F32)
        for j in range(NY):
            row += jnp.where(lax.div(lane[0:1, :], CAP) == 4 * c + j, gpret[j], 0.0)
        row = jnp.broadcast_to(row, (F, F))
        for k in range(2):
            hit = jnp.where(posc[k] == lane + x * F, row, 0.0)
            col = jnp.sum(hit, axis=1, keepdims=True)
            gg[t, k : k + 1, :] = jnp.sum(
                jnp.where(eye, jnp.broadcast_to(col, (F, F)), 0.0), axis=0, keepdims=True
            )
        for i in range(1, 2 * NX):
            remote(
                gg.at[t], gg.at[t], ggsem.at[0], ggsem.at[1], e, lax.rem(t + i, 2 * NX)
            ).start()

    def scale(h):
        @pl.loop(0, D // 256)
        def _(n):
            cols = full_ds(n * 256, 256)
            rh = slice(256 * h, 256 * h + 256)
            scaled[rh, cols] = (wcol[rh, 0:1] * rows[1, rh, cols].astype(F32)).astype(BF16)

    def inputs_grad(h):
        rh = slice(256 * h, 256 * h + 256)

        @pl.loop(0, 3)
        def _(n):
            cols = full_ds(n * 512, 512)
            ip[rh, cols] = lax.dot_general(
                pgrad[rh, :], win[cols, :], (((1,), (1,)), ((), ())), preferred_element_type=F32
            ).astype(BF16)

        other = full_ds((2 * h + 1 - c) * F, F)
        remote(ip.at[other, :], sibrecv.at[h], sibsem.at[0], sibsem.at[1 + h], e, sib).start()

    def ring1(h):
        wait_recv(sibrecv.at[h], sibsem.at[1 + h])
        own = full_ds((2 * h + c) * F, F)
        cs[h] = (ip[own, :].astype(F32) + sibrecv[h].astype(F32)).astype(BF16)
        oc = full_ds(xo * DX, DX)
        remote(cs.at[h, 0:64, oc], r1.at[h, 0], rsem.at[0], rsem.at[2 + h], e, right).start()
        remote(cs.at[h, 64:128, oc], r1.at[h, 1], rsem.at[1], rsem.at[4 + h], e, left).start()

    def ring2(h):
        wait_recv(r1.at[h, 0], rsem.at[2 + h])
        rc = full_ds(xr * DX, DX)
        s2[h, 0, 0:64, :] = (cs[h, 0:64, rc].astype(F32) + r1[h, 0].astype(F32)).astype(BF16)
        s2[h, 0, 64:128, :] = cs[h, 64:128, rc]
        remote(s2.at[h, 0], r2.at[h, 0], rsem.at[6], rsem.at[8 + h], e, right).start()
        wait_recv(r1.at[h, 1], rsem.at[4 + h])
        lc = full_ds(xl * DX, DX)
        s2[h, 1, 64:128, :] = (cs[h, 64:128, lc].astype(F32) + r1[h, 1].astype(F32)).astype(BF16)
        s2[h, 1, 0:64, :] = cs[h, 0:64, lc]
        remote(s2.at[h, 1], r2.at[h, 1], rsem.at[7], rsem.at[10 + h], e, left).start()

    def ring3(h):
        wait_recv(r2.at[h, 0], rsem.at[8 + h])
        wait_recv(r2.at[h, 1], rsem.at[10 + h])
        fin[h] = (
            cs[h, :, xcols].astype(F32) + r2[h, 0].astype(F32) + r2[h, 1].astype(F32)
        ).astype(BF16)

        for q in range(8):
            blk = slice(q * CAP, q * CAP + CAP)
            i = 16 * h + q

            def send():
                to = jnp.where(c == 0, behind(i), behind(i + 8))
                remote(
                    fin.at[h, blk, :], ret.at[h, blk, :], retsem.at[0], retsem.at[1 + h], to, t
                ).start()

            if i == 0:

                @pl.when(c == 0)
                def _():
                    ret[0, 0:CAP, :] = fin[0, 0:CAP, :]

                pl.when(c == 1)(send)
            else:
                send()

    def first_grad(lo, hi):
        @pl.loop(lo, hi)
        def _(m):
            cols = full_ds(m * 256, 256)
            wig[cols, :] = lax.dot_general(
                rows[0, :, cols], pgrad[...], (((0,), (0,)), ((), ())), preferred_element_type=F32
            ).astype(BF16)

    def second_grad(lo, hi):
        @pl.loop(lo, hi)
        def _(m):
            cols = full_ds(m * 256, 256)
            for n in range(2):
                nc = slice(n * 768, n * 768 + 768)
                wog[cols, nc] = lax.dot_general(
                    hidden[:, cols], scaled[:, nc], (((0,), (0,)), ((), ())),
                    preferred_element_type=F32,
                ).astype(BF16)

    spread(0)
    issue(2)
    spread(1)
    relay(0)
    issue(3)
    spread(2)
    relay(1)
    opposite(0)

    share = remote(grecv, grecv, gsem.at[1], gsem.at[2], e, sib)

    @pl.when(c == 1)
    def _():
        wait_recv(grecv.at[1:NE], gsem.at[0])
        share.start()

    spread(3)
    relay(2)
    opposite(1)

    @pl.when(c == 0)
    def _():
        share.wait_recv()

    for g in range(4):
        weigh(g)
    for load in loads[6:]:
        load.wait()
    from_sibling(0)
    from_sibling(1)
    work(0)
    relay(3)
    opposite(2)
    inputs_grad(0)
    opposite(3)
    scale(0)
    ring1(0)
    from_sibling(2)
    from_sibling(3)
    work(1)
    ring2(0)
    inputs_grad(1)
    ring3(0)
    scale(1)
    first_grad(0, 2)
    ring1(1)
    gates_on()
    first_grad(2, 5)
    ring2(1)
    first_grad(5, 6)
    second_grad(0, 2)
    ring3(1)
    second_grad(2, 3)

    @pl.when(c == 0)
    def _():
        wait_recv(ret.at[0, CAP:F, :], retsem.at[1])

    @pl.when(c == 1)
    def _():
        wait_recv(ret.at[0], retsem.at[1])

    wait_recv(ret.at[1], retsem.at[2])
    picks = []
    for h in range(2):
        slot = lane + (2 * h + c) * F
        picks.append(
            jnp.where((posc[0] == slot) | (posc[1] == slot), 1.0, 0.0).astype(BF16)
        )
    pmg[...] = jnp.dot(picks[0], ret[0], preferred_element_type=F32) + jnp.dot(
        picks[1], ret[1], preferred_element_type=F32
    )
    swap = remote(pmg, pmr, pmsem.at[0], pmsem.at[1], e, sib)
    swap.start()
    gates_home()
    swap.wait_recv()
    mgx[16 : 16 + F, :] = cot[:, xcols].astype(F32) + (pmg[...] + pmr[...])

    def gather_own(r, sem):
        remote(r, r, sem.at[0], sem.at[3], e, facing).start()
        remote(r, r, sem.at[0], sem.at[1], e, right).start()
        remote(r, r, sem.at[0], sem.at[2], e, left).start()
        remote(r, r, sem.at[4], sem.at[5], e, sib).start()

    def gather_rest(view, sem):
        for k, xs in ((1, xl), (2, xr), (3, xo)):
            r = view(xs)
            wait_recv(r, sem.at[k])
            remote(r, r, sem.at[4], sem.at[5], e, sib).start()

    @pl.when(c == 0)
    def _():
        up = remote(
            mgx.at[F : F + 16, :], mgx.at[0:16, :], mhsem.at[0], mhsem.at[1], after, t
        )
        down = remote(
            mgx.at[16:32, :], mgx.at[16 + F : EXT, :], mhsem.at[2], mhsem.at[3], before, t
        )
        up.start()
        down.start()
        up.wait_recv()
        down.wait_recv()

        for q in range(NQ):
            tile = full_ds(x * DX + q * 128, 128)
            fgall[:, tile] = conv(mgx, q, True).astype(BF16)
            gather_own(fgall.at[:, tile], fgsem)
        gather_rest(lambda xs: fgall.at[:, full_ds(xs * DX, DX)], fgsem)
        wait_recv(kfull, kfsem.at[5])
        wait_send(fgall.at[:, 0 : 3 * DX], fgsem.at[0])
        wait_send(fgall, fgsem.at[4])
        up.wait_send()
        down.wait_send()

    @pl.when(c == 1)
    def _():
        kg[...] = jnp.zeros_like(kg)
        for j in range(NE):
            if j < KW:
                near = sx[j + 1 : j + 1 + F, :] == sx[16 : 16 + F, :]
                for q in range(NQ):
                    cols = slice(q * 128, q * 128 + 128)
                    prod = jnp.where(
                        near, fx[j + 1 : j + 1 + F, cols] * mgx[16 : 16 + F, cols], 0.0
                    )
                    kg[j, q : q + 1, :] = jnp.sum(prod, axis=0, keepdims=True)

            @pl.when(e == j)
            def _():
                krecv[j] = kg[j]

            @pl.when(e != j)
            def _():
                remote(kg.at[j], krecv.at[e], ksem.at[0], ksem.at[1], j, t).start()

        wait_recv(krecv.at[1:NE], ksem.at[1])
        kred[...] = jnp.sum(krecv[...], axis=0)
        kfull[x, e] = kred[...]
        for i in range(1, NE):
            remote(kred, kfull.at[x, e], ksem.at[2], ksem.at[3], ahead(i), t).start()
        wait_recv(kfull.at[x, 1:NE], ksem.at[3])
        gather_own(kfull.at[x], kfsem)
        gather_rest(lambda xs: kfull.at[xs], kfsem)
        wait_recv(fgall, fgsem.at[5])
        wait_send(kg.at[1:NE], ksem.at[0])
        wait_send(kg.at[1:NE], ksem.at[2])
        wait_send(kfull.at[0:3], kfsem.at[0])
        wait_send(kfull, kfsem.at[4])

    wait_recv(gg.at[1 : 2 * NX], ggsem.at[1])
    gg_out[...] = jnp.sum(gg[...], axis=0)
    fg_out[...] = fgall[...]
    for xs in range(NX):
        for q in range(NQ):
            kg_out[:, xs * DX + q * 128 : xs * DX + q * 128 + 128] = kfull[xs, 0:KW, q, :]

    halo_up.wait_send()
    halo_down.wait_send()
    wait_send(sendbuf.at[CAP:SLOTS, :], asend.at[0])

    @pl.when(c == 1)
    def _():
        wait_send(grecv.at[1:NE], asend.at[1])
        share.wait_send()

    wait_send(rows.at[c, :, xcols], xsend.at[0])
    wait_send(rows.at[c, :, xcols], xsend.at[1])
    wait_send(rows.at[c, :, xcols], xsend.at[2])
    wait_send(rows.at[c], ssend.at[0])
    wait_send(gpx.at[1 : 2 * NX], gpsem.at[0])

    @pl.when(t == 0)
    def _():
        wait_send(gpret.at[1:NY], gpsem.at[2])

    @pl.when(t > 0)
    def _():
        wait_send(gpret, gpsem.at[2])

    wait_send(sibrecv, sibsem.at[0])
    wait_send(r1.at[:, 0], rsem.at[0])
    wait_send(r1.at[:, 1], rsem.at[1])
    wait_send(s2.at[:, 0], rsem.at[6])
    wait_send(s2.at[:, 1], rsem.at[7])

    @pl.when(c == 0)
    def _():
        wait_send(ip.at[CAP : 2 * F, 0:DX], retsem.at[0])

    @pl.when(c == 1)
    def _():
        wait_send(ip.at[0 : 2 * F, 0:DX], retsem.at[0])

    swap.wait_send()
    wait_send(gg.at[1 : 2 * NX], ggsem.at[0])


def write_out(*refs):
    copies = [pltpu.make_async_copy(refs[k], refs[5 + k], refs[10].at[k]) for k in range(5)]
    for copy in copies:
        copy.start()
    for copy in copies:
        copy.wait()


def on_device(frames, cotangent, segment_ids, kernel, expert_ids, gates, w_in, w_out):
    vmem = pl.BlockSpec(memory_space=pltpu.VMEM)
    hbm = pl.BlockSpec(memory_space=pltpu.HBM)
    dma = pltpu.SemaphoreType.DMA
    V = pltpu.VMEM
    scratch = dict(
        frames=V((F, D), BF16),
        cot=V((F, D), BF16),
        seg=V((1, F), jnp.int32),
        kern=V((KW, D), F32),
        ids=V((2, F), jnp.int32),
        gates=V((2, F), BF16),
        win=V((D, HS), BF16),
        wout=V((HS, D), BF16),
        rows=V((2, SLOTS, D), BF16),
        sendbuf=V((SLOTS, DX), BF16),
        src=V((F, DX), BF16),
        hs=V((2, 16, DX + 128), BF16),
        hr=V((2, 16, DX + 128), BF16),
        fx=V((EXT, DX), F32),
        sx=V((EXT, 128), F32),
        gsend=V((4, 1, 128), F32),
        grecv=V((NE, 1, 128), F32),
        wcol=V((SLOTS, 128), F32),
        scaled=V((SLOTS, D), BF16),
        hidden=V((SLOTS, HS), BF16),
        pgrad=V((SLOTS, HS), BF16),
        gacc=V((SLOTS, 128), F32),
        gpsend=V((4, 1, 128), F32),
        gpx=V((2 * NX, 1, 128), F32),
        gprow=V((1, 1, 128), F32),
        gpret=V((NY, 1, 128), F32),
        ip=V((SLOTS, D), BF16),
        sibrecv=V((2, F, D), BF16),
        cs=V((2, F, D), BF16),
        r1=V((2, 2, F // 2, DX), BF16),
        s2=V((2, 2, F, DX), BF16),
        r2=V((2, 2, F, DX), BF16),
        fin=V((2, F, DX), BF16),
        ret=V((2, F, DX), BF16),
        pmg=V((F, DX), F32),
        pmr=V((F, DX), F32),
        mgx=V((EXT, DX), F32),
        fgall=V((F, D), BF16),
        kg=V((NE, 4, 128), F32),
        krecv=V((NE, 4, 128), F32),
        kred=V((4, 128), F32),
        kfull=V((NX, NE, 4, 128), F32),
        gg=V((2 * NX, 2, 128), F32),
        posr=V((2, F, F), jnp.int32),
        posc=V((2, F, F), jnp.int32),
        lsem=dma((8,)),
        hsem=dma((4,)),
        asend=dma((2,)),
        arecv=dma((4,)),
        gsem=dma((3,)),
        xsend=dma((3,)),
        ssend=dma((1,)),
        fl=dma((4,)),
        fr=dma((4,)),
        fo=dma((4,)),
        fs=dma((4,)),
        gpsem=dma((4,)),
        sibsem=dma((3,)),
        rsem=dma((12,)),
        retsem=dma((3,)),
        pmsem=dma((2,)),
        mhsem=dma((4,)),
        fgsem=dma((6,)),
        ksem=dma((4,)),
        kfsem=dma((6,)),
        ggsem=dma((2,)),
    )
    made = pl.pallas_call(
        body,
        out_shape=(
            V((F, D), BF16),
            V((KW, D), F32),
            V((D, HS), BF16),
            V((HS, D), BF16),
            V((2, F), F32),
        ),
        in_specs=[hbm] * 8,
        out_specs=(vmem,) * 5,
        scratch_shapes=list(scratch.values()),
        compiler_params=pltpu.CompilerParams(
            collective_id=0, has_side_effects=True, vmem_limit_bytes=56 * 1024 * 1024
        ),
    )(
        frames,
        cotangent,
        segment_ids.reshape(1, F),
        kernel,
        expert_ids.T,
        gates.T,
        w_in[0],
        w_out[0],
    )
    fg, kg, wig, wog, gg = pl.pallas_call(
        write_out,
        out_shape=tuple(pltpu.HBM(v.shape, v.dtype) for v in made),
        in_specs=[vmem] * 5,
        out_specs=(hbm,) * 5,
        scratch_shapes=[dma((5,))],
        compiler_params=pltpu.CompilerParams(vmem_limit_bytes=2 * 1024 * 1024),
    )(*made)
    return fg, kg, wig[None], wog[None], gg.T


def solution(mesh):
    return jax.shard_map(
        on_device,
        mesh=mesh,
        in_specs=(
            P("expert", None),
            P("expert", None),
            P("expert"),
            P(),
            P("expert", None),
            P("expert", None),
            P("expert", None, "tensor"),
            P("expert", "tensor", None),
        ),
        out_specs=(
            P("expert", None),
            P(),
            P("expert", None, "tensor"),
            P("expert", "tensor", None),
            P("expert", None),
        ),
        check_vma=False,
    )
```

```python
import jax
import jax.numpy as jnp
from jax import lax
from jax.experimental import pallas as pl
from jax.experimental.pallas import tpu as pltpu
from jax.sharding import PartitionSpec as P

MESH = pl.DeviceIdType.MESH
F32 = jnp.float32
BF16 = jnp.bfloat16
NZ, NY, NX = 8, 4, 4
NE = NZ * NY
F = 128
D = 1536
HS = 768
KW = 31
CAP = 16
SLOTS = NE * CAP
DX = D // NX
NQ = DX // 128
EXT = F + 32


def full_ds(start, size):
    return pl.ds(pl.multiple_of(start, 128), size)


def body(
    frames_in, cot_in, seg_in, kern_in, ids_in, gates_in, w_in, w_out,
    fg_out, kg_out, wig, wog, gg_out,
    frames, cot, seg, kern, ids, gates,
    win, wout, rows, sendbuf, src, hs, hr, fx, fx2, sx, gsend, grecv, wcol,
    scaled, hidden, pgrad, gacc, gpsend, gpx, gprow, gpret, ip, sibrecv, cs, r1, s2, r2, fin, ret,
    pmg, pmr, mgx, fgall, kg, krecv, kz, kfull, gg, posr, posc,
    lsem, hsem, asend, arecv, gsem, xsend, ssend, fl, fr, fs, gpsem, sibsem, rsem,
    retsem, pmsem, mhsem, fgsem, ksem, kfsem, ggsem,
):
    e = lax.axis_index("expert")
    t = lax.axis_index("tensor")
    z, y = lax.div(e, NY), lax.rem(e, NY)
    x, c = lax.div(t, 2), lax.rem(t, 2)
    sib = t + 1 - 2 * c
    xr, xl, xo = lax.rem(x + 1, NX), lax.rem(x + 3, NX), lax.rem(x + 2, NX)
    right, left, facing = xr * 2 + c, xl * 2 + c, xo * 2 + c
    xcols = full_ds(x * DX, DX)

    zt = [lax.rem(z + k, NZ) * NY for k in range(NZ)]
    yt = [lax.rem(y + k, NY) for k in range(NY)]

    def offset(i):
        p = i // NY
        return ((p + 1) // 2 if p % 2 else (NZ - p // 2) % NZ), i % NY

    def ahead(i):
        dz, dy = offset(i)
        return zt[dz] + yt[dy]

    def behind(i):
        dz, dy = offset(i)
        return zt[(NZ - dz) % NZ] + yt[(NY - dy) % NY]

    def remote(s, d, ss, rs, ee, tt):
        return pltpu.make_async_remote_copy(
            src_ref=s, dst_ref=d, send_sem=ss, recv_sem=rs, device_id=(ee, tt), device_id_type=MESH
        )

    def wait_recv(ref, sem):
        remote(ref, ref, sem, sem, e, sib).wait_recv()

    def wait_send(ref, sem):
        remote(ref, ref, sem, sem, e, sib).wait_send()

    barrier = pltpu.get_barrier_semaphore()

    for i in range(1, NE):
        pl.semaphore_signal(barrier, inc=1, device_id=(ahead(i), t), device_id_type=MESH)
    for i in range(1, 2 * NX):
        pl.semaphore_signal(
            barrier, inc=1, device_id=(e, lax.rem(t + i, 2 * NX)), device_id_type=MESH
        )
    for tt in (right, left, facing):
        for m in range(1, NY):
            pl.semaphore_signal(
                barrier, inc=1, device_id=(z * NY + yt[m], tt), device_id_type=MESH
            )
    pairs = (
        (ids_in, ids), (gates_in, gates), (seg_in, seg), (frames_in, frames), (cot_in, cot),
        (kern_in, kern), (w_in, win), (w_out, wout),
    )
    loads = [pltpu.make_async_copy(a, b, lsem.at[k]) for k, (a, b) in enumerate(pairs)]
    for load in loads:
        load.start()
    for load in loads[:3]:
        load.wait()

    lane = lax.broadcasted_iota(jnp.int32, (F, F), 1)
    sub = lax.broadcasted_iota(jnp.int32, (F, F), 0)
    eye = lane == sub
    idr = [jnp.broadcast_to(ids[k : k + 1, :], (F, F)).astype(F32) for k in range(2)]
    idc = [v.T for v in idr]

    def place(idf, rank):
        idv = idf.astype(jnp.int32)
        dz = (idv // NY - z + NZ) & (NZ - 1)
        dy = (idv - (idv // NY) * NY - y + NY) & (NY - 1)
        p = jnp.maximum(jnp.where(dz <= NZ // 2, 2 * dz - 1, 2 * NZ - 2 * dz), 0)
        return (p * NY + dy) * CAP + rank.astype(jnp.int32)

    for k in range(2):
        hits = jnp.where(idc[0] == idr[k], 1.0, 0.0) + jnp.where(idc[1] == idr[k], 1.0, 0.0)
        rank = jnp.sum(jnp.where(sub < lane, hits, 0.0), axis=0, keepdims=True)
        posr[k] = place(idr[k], jnp.broadcast_to(rank, (F, F)))
        hits = jnp.where(idr[0] == idc[k], 1.0, 0.0) + jnp.where(idr[1] == idc[k], 1.0, 0.0)
        rank = jnp.sum(jnp.where(lane < sub, hits, 0.0), axis=1, keepdims=True)
        posc[k] = place(idc[k], jnp.broadcast_to(rank, (F, F)))

    for g in range(4):
        total = jnp.zeros((1, F), F32)
        for k in range(2):
            gcol = jnp.broadcast_to(gates[k : k + 1, :].astype(F32), (F, F)).T
            total += jnp.sum(
                jnp.where(posc[k] == lane + g * F, gcol, 0.0), axis=0, keepdims=True
            )
        gsend[g] = total

    @pl.when(c == 1)
    def _():
        grecv[0] = gsend[0]

    for load in loads[3:6]:
        load.wait()
    segr = jnp.broadcast_to(seg[...], (F, F)).astype(F32)
    segc = segr.T
    sx[16 : 16 + F, :] = segc
    ocols = full_ds(xo * DX, DX)
    for k, rs in enumerate((slice(0, 16), slice(F - 16, F))):
        hs[k, :, 0:DX] = frames[rs, xcols]
        hs[k, :, DX : 2 * DX] = frames[rs, ocols]
        hs[k, :, 2 * DX : 2 * DX + 128] = segc[rs].astype(BF16)

    @pl.loop(0, NQ)
    def _(q):
        tile = full_ds(q * 128, 128)
        fx[16 : 16 + F, tile] = frames[:, full_ds(x * DX + q * 128, 128)].astype(F32)
        fx2[16 : 16 + F, tile] = frames[:, full_ds(xo * DX + q * 128, 128)].astype(F32)

    pl.semaphore_wait(barrier, NE - 1 + 2 * NX - 1 + 3 * (NY - 1))

    before, after = lax.rem(e + NE - 1, NE), lax.rem(e + 1, NE)
    halo_up = remote(hs.at[1], hr.at[0], hsem.at[0], hsem.at[1], after, t)
    halo_down = remote(hs.at[0], hr.at[1], hsem.at[2], hsem.at[3], before, t)
    halo_up.start()
    halo_down.start()

    def take_halo():
        halo_up.wait_recv()
        halo_down.wait_recv()
        for k, rs in enumerate((slice(0, 16), slice(16 + F, EXT))):
            fx[rs, :] = hr[k, :, 0:DX].astype(F32)
            fx2[rs, :] = hr[k, :, DX : 2 * DX].astype(F32)
        sx[0:16, :] = jnp.where(e == 0, -1.0, hr[0, :, 2 * DX : 2 * DX + 128].astype(F32))
        sx[16 + F : EXT, :] = jnp.where(
            e == NE - 1, -1.0, hr[1, :, 2 * DX : 2 * DX + 128].astype(F32)
        )

    def conv(ext, xs, q, backwards):
        cols = full_ds(q * 128, 128)
        kcols = full_ds(xs * DX + q * 128, 128)
        acc = jnp.zeros((F, 128), F32)
        own = sx[16 : 16 + F, :]
        for j in range(KW):
            tap = kern[KW - 1 - j if backwards else j, kcols].reshape(1, 128)
            acc += jnp.where(sx[j + 1 : j + 1 + F, :] == own, ext[j + 1 : j + 1 + F, cols] * tap, 0.0)
        return acc + ext[16 : 16 + F, cols]

    def source(first, ext, xs):
        @pl.when(c == 0)
        def _():
            if first:
                take_halo()

            @pl.loop(0, NQ)
            def _(q):
                src[:, full_ds(q * 128, 128)] = conv(ext, xs, q, False).astype(BF16)

        @pl.when(c == 1)
        def _():
            src[...] = cot[:, full_ds(xs * DX, DX)]

    def issue(part, xs, g):
        cols = full_ds(xs * DX, DX)
        slot = sub + g * F
        onehot = jnp.where((posr[0] == slot) | (posr[1] == slot), 1.0, 0.0).astype(BF16)
        sendbuf[part, g * F : g * F + F, :] = jnp.dot(
            onehot, src[...], preferred_element_type=F32
        ).astype(BF16)
        for i in range(max(8 * g, 1), 8 * g + 8):
            blk = slice(i * CAP, i * CAP + CAP)
            remote(
                sendbuf.at[part, blk, :], rows.at[c, blk, cols], asend.at[2 * part],
                arecv.at[4 * part + g], ahead(i), t,
            ).start()
        if g == 0:
            rows[c, 0:CAP, cols] = sendbuf[part, 0:CAP, :]

    source(True, fx, x)
    for g in range(4):
        issue(0, x, g)
    source(False, fx2, xo)
    for g in range(4):
        issue(1, xo, g)

    @pl.when(c == 1)
    def _():
        for i in range(1, NE):
            remote(
                gsend.at[i // 8], grecv.at[i], asend.at[1], gsem.at[0], ahead(i), t
            ).start()

    @pl.when(c == 1)
    def _():
        take_halo()

    def region(g, xs):
        return rows.at[c, g * F : g * F + F, full_ds(xs * DX, DX)]

    def to_sibling(g, xs):
        r = region(g, xs)
        remote(r, r, ssend.at[0], fs.at[g], e, sib).start()

    def arrive(part, xs, g):
        if g == 0:
            wait_recv(rows.at[c, CAP:F, full_ds(xs * DX, DX)], arecv.at[4 * part])
        else:
            wait_recv(region(g, xs), arecv.at[4 * part + g])

    def spread(g):
        arrive(0, x, g)
        r = region(g, x)
        remote(r, r, xsend.at[0], fl.at[g], e, right).start()
        remote(r, r, xsend.at[1], fr.at[g], e, left).start()
        to_sibling(g, x)

    def relay(g):
        wait_recv(region(g, xl), fl.at[g])
        to_sibling(g, xl)
        wait_recv(region(g, xr), fr.at[g])
        to_sibling(g, xr)

    def opposite(g):
        arrive(1, xo, g)
        to_sibling(g, xo)

    def from_sibling(g):
        wait_recv(rows.at[1 - c, g * F : g * F + F, :], fs.at[g])

    def weigh(g):
        parts = [jnp.broadcast_to(grecv[8 * g + q], (CAP, F)) for q in range(8)]
        w = jnp.sum(jnp.where(eye, jnp.concatenate(parts, axis=0), 0.0), axis=1, keepdims=True)
        wcol[g * F : g * F + F, :] = jnp.broadcast_to(w, (F, 128))

    def work(h):
        hr_ = slice(256 * h, 256 * h + 256)
        gacc[hr_, :] = jnp.zeros((256, 128), F32)

        @pl.loop(0, HS // 256)
        def _(n):
            cols = full_ds(n * 256, 256)
            pre = jnp.dot(rows[0, hr_, :], win[:, cols], preferred_element_type=F32)
            back = lax.dot_general(
                rows[1, hr_, :], wout[cols, :], (((1,), (1,)), ((), ())), preferred_element_type=F32
            )
            sig = jax.nn.sigmoid(pre)
            hid = (pre * sig).astype(BF16)
            hidden[hr_, cols] = hid
            prod = hid.astype(F32) * back
            gacc[hr_, :] += prod[:, 0:128] + prod[:, 128:256]
            w = wcol[hr_, 0:1]
            pgrad[hr_, cols] = (back * w * (sig * (1.0 + pre * (1.0 - sig)))).astype(BF16)

        for g in (2 * h, 2 * h + 1):
            part = jnp.sum(gacc[g * F : g * F + F, :], axis=1, keepdims=True)
            row = jnp.sum(
                jnp.where(eye, jnp.broadcast_to(part, (F, F)), 0.0), axis=0, keepdims=True
            )
            gpsend[g] = row

        for tt in range(4 * h, 4 * h + 4):

            @pl.when(t == tt)
            def _():
                gpx[tt] = gpsend[tt // 2]

            @pl.when(t != tt)
            def _():
                remote(
                    gpsend.at[tt // 2], gpx.at[t], gpsem.at[0], gpsem.at[1], e, tt
                ).start()

    def gates_on():
        wait_recv(gpx.at[1 : 2 * NX], gpsem.at[1])
        gprow[0] = jnp.sum(gpx[...], axis=0)
        dz = c * (x + 1) + (1 - c) * lax.rem(NZ - x, NZ)
        zz = lax.rem(z + NZ - dz, NZ) * NY

        @pl.when(t == 0)
        def _():
            gpret[0] = gprow[0]

        @pl.when(t > 0)
        def _():
            remote(gprow.at[0], gpret.at[0], gpsem.at[2], gpsem.at[3], zz + yt[0], t).start()

        for j in range(1, NY):
            remote(
                gprow.at[0], gpret.at[j], gpsem.at[2], gpsem.at[3], zz + yt[NY - j], t
            ).start()

    def gates_home():
        @pl.when(t == 0)
        def _():
            wait_recv(gpret.at[1:NY], gpsem.at[3])

        @pl.when(t > 0)
        def _():
            wait_recv(gpret, gpsem.at[3])

        row = jnp.zeros((1, F), F32)
        for j in range(NY):
            row += jnp.where(lax.div(lane[0:1, :], CAP) == 4 * c + j, gpret[j], 0.0)
        row = jnp.broadcast_to(row, (F, F))
        for k in range(2):
            hit = jnp.where(posc[k] == lane + x * F, row, 0.0)
            col = jnp.sum(hit, axis=1, keepdims=True)
            gg[t, k : k + 1, :] = jnp.sum(
                jnp.where(eye, jnp.broadcast_to(col, (F, F)), 0.0), axis=0, keepdims=True
            )
        for i in range(1, 2 * NX):
            remote(
                gg.at[t], gg.at[t], ggsem.at[0], ggsem.at[1], e, lax.rem(t + i, 2 * NX)
            ).start()

    def scale(h):
        @pl.loop(0, D // 256)
        def _(n):
            cols = full_ds(n * 256, 256)
            rh = slice(256 * h, 256 * h + 256)
            scaled[rh, cols] = (wcol[rh, 0:1] * rows[1, rh, cols].astype(F32)).astype(BF16)

    def inputs_grad(h):
        rh = slice(256 * h, 256 * h + 256)

        @pl.loop(0, 3)
        def _(n):
            cols = full_ds(n * 512, 512)
            ip[rh, cols] = lax.dot_general(
                pgrad[rh, :], win[cols, :], (((1,), (1,)), ((), ())), preferred_element_type=F32
            ).astype(BF16)

        other = full_ds((2 * h + 1 - c) * F, F)
        remote(ip.at[other, :], sibrecv.at[h], sibsem.at[0], sibsem.at[1 + h], e, sib).start()

    def ring1(h):
        wait_recv(sibrecv.at[h], sibsem.at[1 + h])
        own = full_ds((2 * h + c) * F, F)
        cs[h] = (ip[own, :].astype(F32) + sibrecv[h].astype(F32)).astype(BF16)
        oc = full_ds(xo * DX, DX)
        remote(cs.at[h, 0:64, oc], r1.at[h, 0], rsem.at[0], rsem.at[2 + h], e, right).start()
        remote(cs.at[h, 64:128, oc], r1.at[h, 1], rsem.at[1], rsem.at[4 + h], e, left).start()

    def ring2(h):
        wait_recv(r1.at[h, 0], rsem.at[2 + h])
        rc = full_ds(xr * DX, DX)
        s2[h, 0, 0:64, :] = (cs[h, 0:64, rc].astype(F32) + r1[h, 0].astype(F32)).astype(BF16)
        s2[h, 0, 64:128, :] = cs[h, 64:128, rc]
        remote(s2.at[h, 0], r2.at[h, 0], rsem.at[6], rsem.at[8 + h], e, right).start()
        wait_recv(r1.at[h, 1], rsem.at[4 + h])
        lc = full_ds(xl * DX, DX)
        s2[h, 1, 64:128, :] = (cs[h, 64:128, lc].astype(F32) + r1[h, 1].astype(F32)).astype(BF16)
        s2[h, 1, 0:64, :] = cs[h, 0:64, lc]
        remote(s2.at[h, 1], r2.at[h, 1], rsem.at[7], rsem.at[10 + h], e, left).start()

    def ring3(h):
        wait_recv(r2.at[h, 0], rsem.at[8 + h])
        wait_recv(r2.at[h, 1], rsem.at[10 + h])
        fin[h] = (
            cs[h, :, xcols].astype(F32) + r2[h, 0].astype(F32) + r2[h, 1].astype(F32)
        ).astype(BF16)

        for q in range(8):
            blk = slice(q * CAP, q * CAP + CAP)
            i = 16 * h + q

            def send():
                to = jnp.where(c == 0, behind(i), behind(i + 8))
                remote(
                    fin.at[h, blk, :], ret.at[h, blk, :], retsem.at[0], retsem.at[1 + h], to, t
                ).start()

            if i == 0:

                @pl.when(c == 0)
                def _():
                    ret[0, 0:CAP, :] = fin[0, 0:CAP, :]

                pl.when(c == 1)(send)
            else:
                send()

    def first_grad(lo, hi):
        @pl.loop(lo, hi)
        def _(m):
            cols = full_ds(m * 256, 256)
            wig[cols, :] = lax.dot_general(
                rows[0, :, cols], pgrad[...], (((0,), (0,)), ((), ())), preferred_element_type=F32
            ).astype(BF16)

    def second_grad(lo, hi):
        @pl.loop(lo, hi)
        def _(m):
            cols = full_ds(m * 256, 256)
            for n in range(2):
                nc = slice(n * 768, n * 768 + 768)
                wog[cols, nc] = lax.dot_general(
                    hidden[:, cols], scaled[:, nc], (((0,), (0,)), ((), ())),
                    preferred_element_type=F32,
                ).astype(BF16)

    spread(0)
    spread(1)
    spread(2)
    spread(3)
    opposite(0)
    relay(0)
    opposite(1)
    relay(1)

    share = remote(grecv, grecv, gsem.at[1], gsem.at[2], e, sib)

    @pl.when(c == 1)
    def _():
        wait_recv(grecv.at[1:NE], gsem.at[0])
        share.start()

    opposite(2)
    relay(2)
    opposite(3)

    @pl.when(c == 0)
    def _():
        share.wait_recv()

    for g in range(4):
        weigh(g)
    for load in loads[6:]:
        load.wait()
    from_sibling(0)
    from_sibling(1)
    work(0)
    relay(3)
    inputs_grad(0)
    scale(0)
    ring1(0)
    from_sibling(2)
    from_sibling(3)
    work(1)
    ring2(0)
    inputs_grad(1)
    ring3(0)
    scale(1)
    first_grad(0, 2)
    ring1(1)
    gates_on()
    first_grad(2, 4)
    ring2(1)
    first_grad(4, 6)
    ring3(1)
    second_grad(0, 3)

    @pl.when(c == 0)
    def _():
        wait_recv(ret.at[0, CAP:F, :], retsem.at[1])

    @pl.when(c == 1)
    def _():
        wait_recv(ret.at[0], retsem.at[1])

    wait_recv(ret.at[1], retsem.at[2])
    picks = []
    for h in range(2):
        slot = lane + (2 * h + c) * F
        picks.append(
            jnp.where((posc[0] == slot) | (posc[1] == slot), 1.0, 0.0).astype(BF16)
        )
    pmg[...] = jnp.dot(picks[0], ret[0], preferred_element_type=F32) + jnp.dot(
        picks[1], ret[1], preferred_element_type=F32
    )
    swap = remote(pmg, pmr, pmsem.at[0], pmsem.at[1], e, sib)
    swap.start()
    gates_home()
    swap.wait_recv()
    mgx[16 : 16 + F, :] = cot[:, xcols].astype(F32) + (pmg[...] + pmr[...])

    def gather_own(r, sem):
        remote(r, r, sem.at[0], sem.at[3], e, facing).start()
        remote(r, r, sem.at[0], sem.at[1], e, right).start()
        remote(r, r, sem.at[0], sem.at[2], e, left).start()
        remote(r, r, sem.at[4], sem.at[5], e, sib).start()

    def gather_rest(view, sem):
        for k, xs in ((1, xl), (2, xr), (3, xo)):
            r = view(xs)
            wait_recv(r, sem.at[k])
            remote(r, r, sem.at[4], sem.at[5], e, sib).start()

    @pl.when(c == 0)
    def _():
        up = remote(
            mgx.at[F : F + 16, :], mgx.at[0:16, :], mhsem.at[0], mhsem.at[1], after, t
        )
        down = remote(
            mgx.at[16:32, :], mgx.at[16 + F : EXT, :], mhsem.at[2], mhsem.at[3], before, t
        )
        up.start()
        down.start()
        up.wait_recv()
        down.wait_recv()

        for q in range(NQ):
            tile = full_ds(x * DX + q * 128, 128)
            fgall[:, tile] = conv(mgx, x, q, True).astype(BF16)
            gather_own(fgall.at[:, tile], fgsem)
        gather_rest(lambda xs: fgall.at[:, full_ds(xs * DX, DX)], fgsem)
        wait_recv(kfull, kfsem.at[5])
        wait_send(fgall.at[:, 0 : 3 * DX], fgsem.at[0])
        wait_send(fgall, fgsem.at[4])
        up.wait_send()
        down.wait_send()

    @pl.when(c == 1)
    def _():
        kg[...] = jnp.zeros_like(kg)
        for j in range(NE):
            if j < KW:
                near = sx[j + 1 : j + 1 + F, :] == sx[16 : 16 + F, :]
                for q in range(NQ):
                    cols = slice(q * 128, q * 128 + 128)
                    prod = jnp.where(
                        near, fx[j + 1 : j + 1 + F, cols] * mgx[16 : 16 + F, cols], 0.0
                    )
                    kg[j, q : q + 1, :] = jnp.sum(prod, axis=0, keepdims=True)

            if j % 8 == 7:

                @pl.when(y != j // 8)
                def _():
                    remote(
                        kg.at[j - 7 : j + 1], krecv.at[y], ksem.at[0], ksem.at[1],
                        z * NY + j // 8, t,
                    ).start()

                @pl.when(y == j // 8)
                def _():
                    krecv[y] = kg[j - 7 : j + 1]

        wait_recv(krecv.at[1:NY], ksem.at[1])
        kz[z] = jnp.sum(krecv[...], axis=0)
        for k in range(1, NZ):
            remote(kz.at[z], kz.at[z], ksem.at[2], ksem.at[3], zt[k] + y, t).start()
        wait_recv(kz.at[1:NZ], ksem.at[3])
        own = pl.ds(pl.multiple_of(y * 8, 8), 8)
        kfull[x, own] = jnp.sum(kz[...], axis=0)
        mine = kfull.at[x, own]
        for k, tt in ((3, facing), (1, right), (2, left), (0, t)):
            for m in range(0 if k else 1, NY):
                remote(mine, mine, kfsem.at[4], kfsem.at[k], z * NY + yt[m], tt).start()
        wait_recv(kfull.at[x, 0:24], kfsem.at[0])
        remote(kfull.at[x], kfull.at[x], kfsem.at[6], kfsem.at[5], e, sib).start()
        for k, xs in ((1, xl), (2, xr), (3, xo)):
            wait_recv(kfull.at[xs], kfsem.at[k])
            remote(kfull.at[xs], kfull.at[xs], kfsem.at[6], kfsem.at[5], e, sib).start()
        wait_recv(fgall, fgsem.at[5])
        wait_send(krecv.at[1:NY], ksem.at[0])
        wait_send(kz.at[1:NZ], ksem.at[2])
        wait_send(ip.at[0:320, 0:DX], kfsem.at[4])
        wait_send(kfull, kfsem.at[6])

    wait_recv(gg.at[1 : 2 * NX], ggsem.at[1])
    gg_out[...] = jnp.sum(gg[...], axis=0)
    fg_out[...] = fgall[...]
    for xs in range(NX):
        for q in range(NQ):
            kg_out[:, xs * DX + q * 128 : xs * DX + q * 128 + 128] = kfull[xs, 0:KW, q, :]

    halo_up.wait_send()
    halo_down.wait_send()
    wait_send(sendbuf.at[0, CAP:SLOTS, :], asend.at[0])
    wait_send(sendbuf.at[1, CAP:SLOTS, :], asend.at[2])

    @pl.when(c == 1)
    def _():
        wait_send(grecv.at[1:NE], asend.at[1])
        share.wait_send()

    wait_send(rows.at[c, :, xcols], xsend.at[0])
    wait_send(rows.at[c, :, xcols], xsend.at[1])
    wait_send(rows.at[c], ssend.at[0])
    wait_send(gpx.at[1 : 2 * NX], gpsem.at[0])

    @pl.when(t == 0)
    def _():
        wait_send(gpret.at[1:NY], gpsem.at[2])

    @pl.when(t > 0)
    def _():
        wait_send(gpret, gpsem.at[2])

    wait_send(sibrecv, sibsem.at[0])
    wait_send(r1.at[:, 0], rsem.at[0])
    wait_send(r1.at[:, 1], rsem.at[1])
    wait_send(s2.at[:, 0], rsem.at[6])
    wait_send(s2.at[:, 1], rsem.at[7])

    @pl.when(c == 0)
    def _():
        wait_send(ip.at[CAP : 2 * F, 0:DX], retsem.at[0])

    @pl.when(c == 1)
    def _():
        wait_send(ip.at[0 : 2 * F, 0:DX], retsem.at[0])

    swap.wait_send()
    wait_send(gg.at[1 : 2 * NX], ggsem.at[0])


def write_out(*refs):
    copies = [pltpu.make_async_copy(refs[k], refs[5 + k], refs[10].at[k]) for k in range(5)]
    for copy in copies:
        copy.start()
    for copy in copies:
        copy.wait()


def on_device(frames, cotangent, segment_ids, kernel, expert_ids, gates, w_in, w_out):
    vmem = pl.BlockSpec(memory_space=pltpu.VMEM)
    hbm = pl.BlockSpec(memory_space=pltpu.HBM)
    dma = pltpu.SemaphoreType.DMA
    V = pltpu.VMEM
    scratch = dict(
        frames=V((F, D), BF16),
        cot=V((F, D), BF16),
        seg=V((1, F), jnp.int32),
        kern=V((KW, D), F32),
        ids=V((2, F), jnp.int32),
        gates=V((2, F), BF16),
        win=V((D, HS), BF16),
        wout=V((HS, D), BF16),
        rows=V((2, SLOTS, D), BF16),
        sendbuf=V((2, SLOTS, DX), BF16),
        src=V((F, DX), BF16),
        hs=V((2, 16, 2 * DX + 128), BF16),
        hr=V((2, 16, 2 * DX + 128), BF16),
        fx=V((EXT, DX), F32),
        fx2=V((EXT, DX), F32),
        sx=V((EXT, 128), F32),
        gsend=V((4, 1, 128), F32),
        grecv=V((NE, 1, 128), F32),
        wcol=V((SLOTS, 128), F32),
        scaled=V((SLOTS, D), BF16),
        hidden=V((SLOTS, HS), BF16),
        pgrad=V((SLOTS, HS), BF16),
        gacc=V((SLOTS, 128), F32),
        gpsend=V((4, 1, 128), F32),
        gpx=V((2 * NX, 1, 128), F32),
        gprow=V((1, 1, 128), F32),
        gpret=V((NY, 1, 128), F32),
        ip=V((SLOTS, D), BF16),
        sibrecv=V((2, F, D), BF16),
        cs=V((2, F, D), BF16),
        r1=V((2, 2, F // 2, DX), BF16),
        s2=V((2, 2, F, DX), BF16),
        r2=V((2, 2, F, DX), BF16),
        fin=V((2, F, DX), BF16),
        ret=V((2, F, DX), BF16),
        pmg=V((F, DX), F32),
        pmr=V((F, DX), F32),
        mgx=V((EXT, DX), F32),
        fgall=V((F, D), BF16),
        kg=V((NE, 4, 128), F32),
        krecv=V((NY, 8, 4, 128), F32),
        kz=V((NZ, 8, 4, 128), F32),
        kfull=V((NX, NE, 4, 128), F32),
        gg=V((2 * NX, 2, 128), F32),
        posr=V((2, F, F), jnp.int32),
        posc=V((2, F, F), jnp.int32),
        lsem=dma((8,)),
        hsem=dma((4,)),
        asend=dma((3,)),
        arecv=dma((8,)),
        gsem=dma((3,)),
        xsend=dma((2,)),
        ssend=dma((1,)),
        fl=dma((4,)),
        fr=dma((4,)),
        fs=dma((4,)),
        gpsem=dma((4,)),
        sibsem=dma((3,)),
        rsem=dma((12,)),
        retsem=dma((3,)),
        pmsem=dma((2,)),
        mhsem=dma((4,)),
        fgsem=dma((6,)),
        ksem=dma((4,)),
        kfsem=dma((7,)),
        ggsem=dma((2,)),
    )
    made = pl.pallas_call(
        body,
        out_shape=(
            V((F, D), BF16),
            V((KW, D), F32),
            V((D, HS), BF16),
            V((HS, D), BF16),
            V((2, F), F32),
        ),
        in_specs=[hbm] * 8,
        out_specs=(vmem,) * 5,
        scratch_shapes=list(scratch.values()),
        compiler_params=pltpu.CompilerParams(
            collective_id=0, has_side_effects=True, vmem_limit_bytes=56 * 1024 * 1024
        ),
    )(
        frames,
        cotangent,
        segment_ids.reshape(1, F),
        kernel,
        expert_ids.T,
        gates.T,
        w_in[0],
        w_out[0],
    )
    fg, kg, wig, wog, gg = pl.pallas_call(
        write_out,
        out_shape=tuple(pltpu.HBM(v.shape, v.dtype) for v in made),
        in_specs=[vmem] * 5,
        out_specs=(hbm,) * 5,
        scratch_shapes=[dma((5,))],
        compiler_params=pltpu.CompilerParams(vmem_limit_bytes=2 * 1024 * 1024),
    )(*made)
    return fg, kg, wig[None], wog[None], gg.T


def solution(mesh):
    return jax.shard_map(
        on_device,
        mesh=mesh,
        in_specs=(
            P("expert", None),
            P("expert", None),
            P("expert"),
            P(),
            P("expert", None),
            P("expert", None),
            P("expert", None, "tensor"),
            P("expert", "tensor", None),
        ),
        out_specs=(
            P("expert", None),
            P(),
            P("expert", None, "tensor"),
            P("expert", "tensor", None),
            P("expert", None),
        ),
        check_vma=False,
    )
```

```python
import jax
import jax.numpy as jnp
from jax import lax
from jax.experimental import pallas as pl
from jax.experimental.pallas import tpu as pltpu
from jax.sharding import PartitionSpec as P

MESH = pl.DeviceIdType.MESH
F32 = jnp.float32
BF16 = jnp.bfloat16
NZ, NY, NX = 8, 4, 4
NE = NZ * NY
F = 128
HF = F // 2
D = 1536
HS = 768
KW = 31
CAP = 16
SLOTS = NE * CAP
DX = D // NX
NQ = DX // 128
EXT = F + 32


def full_ds(start, size):
    return pl.ds(pl.multiple_of(start, 128), size)


def body(
    frames_in, cot_in, seg_in, kern_in, ids_in, gates_in, w_in, w_out,
    fg_out, kg_out, wig, wog, gg_out,
    frames, cot, seg, kern, ids, gates,
    win, wout, rows, sendbuf, src, hs, hr, fx, fx2, sx, gsend, grecv, wcol,
    scaled, hidden, pgrad, gacc, gpsend, gpx, gprow, gpret, ip, sibrecv, cs, r1, s2, r2, fin, ret,
    mgx, fgall, kg, krecv, kz, kfull, gg, posr, posc,
    lsem, hsem, asend, arecv, gsem, xsend, ssend, fl, fr, fs, gpsem, sibsem, rsem,
    retsem, mhsem, fgsem, ksem, kfsem, ggsem,
):
    e = lax.axis_index("expert")
    t = lax.axis_index("tensor")
    z, y = lax.div(e, NY), lax.rem(e, NY)
    x, c = lax.div(t, 2), lax.rem(t, 2)
    sib = t + 1 - 2 * c
    xr, xl, xo = lax.rem(x + 1, NX), lax.rem(x + 3, NX), lax.rem(x + 2, NX)
    right, left, facing = xr * 2 + c, xl * 2 + c, xo * 2 + c
    xcols = full_ds(x * DX, DX)

    zt = [lax.rem(z + k, NZ) * NY for k in range(NZ)]
    yt = [lax.rem(y + k, NY) for k in range(NY)]

    def offset(i):
        p = i // NY
        return ((p + 1) // 2 if p % 2 else (NZ - p // 2) % NZ), i % NY

    def ahead(i):
        dz, dy = offset(i)
        return zt[dz] + yt[dy]

    def behind(i):
        dz, dy = offset(i)
        return zt[(NZ - dz) % NZ] + yt[(NY - dy) % NY]

    def remote(s, d, ss, rs, ee, tt):
        return pltpu.make_async_remote_copy(
            src_ref=s, dst_ref=d, send_sem=ss, recv_sem=rs, device_id=(ee, tt), device_id_type=MESH
        )

    def wait_recv(ref, sem):
        remote(ref, ref, sem, sem, e, sib).wait_recv()

    def wait_send(ref, sem):
        remote(ref, ref, sem, sem, e, sib).wait_send()

    barrier = pltpu.get_barrier_semaphore()

    for i in range(1, NE):
        for tt in (t, sib):
            pl.semaphore_signal(barrier, inc=1, device_id=(ahead(i), tt), device_id_type=MESH)
    for i in range(1, 2 * NX):
        pl.semaphore_signal(
            barrier, inc=1, device_id=(e, lax.rem(t + i, 2 * NX)), device_id_type=MESH
        )
    for tt in (right, left, facing, right + sib - t, left + sib - t, facing + sib - t):
        for m in range(1, NY):
            pl.semaphore_signal(
                barrier, inc=1, device_id=(z * NY + yt[m], tt), device_id_type=MESH
            )
    pairs = (
        (ids_in, ids), (gates_in, gates), (seg_in, seg), (frames_in, frames), (cot_in, cot),
        (kern_in, kern), (w_in, win), (w_out, wout),
    )
    loads = [pltpu.make_async_copy(a, b, lsem.at[k]) for k, (a, b) in enumerate(pairs)]
    for load in loads:
        load.start()
    for load in loads[:3]:
        load.wait()

    lane = lax.broadcasted_iota(jnp.int32, (F, F), 1)
    sub = lax.broadcasted_iota(jnp.int32, (F, F), 0)
    eye = lane == sub
    idr = [jnp.broadcast_to(ids[k : k + 1, :], (F, F)).astype(F32) for k in range(2)]
    idc = [v.T for v in idr]

    def place(idf, rank):
        idv = idf.astype(jnp.int32)
        dz = (idv // NY - z + NZ) & (NZ - 1)
        dy = (idv - (idv // NY) * NY - y + NY) & (NY - 1)
        p = jnp.maximum(jnp.where(dz <= NZ // 2, 2 * dz - 1, 2 * NZ - 2 * dz), 0)
        return (p * NY + dy) * CAP + rank.astype(jnp.int32)

    for k in range(2):
        hits = jnp.where(idc[0] == idr[k], 1.0, 0.0) + jnp.where(idc[1] == idr[k], 1.0, 0.0)
        rank = jnp.sum(jnp.where(sub < lane, hits, 0.0), axis=0, keepdims=True)
        posr[k] = place(idr[k], jnp.broadcast_to(rank, (F, F)))
        hits = jnp.where(idr[0] == idc[k], 1.0, 0.0) + jnp.where(idr[1] == idc[k], 1.0, 0.0)
        rank = jnp.sum(jnp.where(lane < sub, hits, 0.0), axis=1, keepdims=True)
        posc[k] = place(idc[k], jnp.broadcast_to(rank, (F, F)))

    for g in range(4):
        total = jnp.zeros((1, F), F32)
        for k in range(2):
            gcol = jnp.broadcast_to(gates[k : k + 1, :].astype(F32), (F, F)).T
            total += jnp.sum(
                jnp.where(posc[k] == lane + g * F, gcol, 0.0), axis=0, keepdims=True
            )
        gsend[g] = total

    @pl.when(c == 1)
    def _():
        grecv[0] = gsend[0]

    for load in loads[3:6]:
        load.wait()
    segr = jnp.broadcast_to(seg[...], (F, F)).astype(F32)
    segc = segr.T
    sx[16 : 16 + F, :] = segc
    ocols = full_ds(xo * DX, DX)
    for k, rs in enumerate((slice(0, 16), slice(F - 16, F))):
        hs[k, :, 0:DX] = frames[rs, xcols]
        hs[k, :, DX : 2 * DX] = frames[rs, ocols]
        hs[k, :, 2 * DX : 2 * DX + 128] = segc[rs].astype(BF16)

    @pl.loop(0, NQ)
    def _(q):
        tile = full_ds(q * 128, 128)
        fx[16 : 16 + F, tile] = frames[:, full_ds(x * DX + q * 128, 128)].astype(F32)
        fx2[16 : 16 + F, tile] = frames[:, full_ds(xo * DX + q * 128, 128)].astype(F32)

    pl.semaphore_wait(barrier, 2 * (NE - 1) + 2 * NX - 1 + 6 * (NY - 1))

    before, after = lax.rem(e + NE - 1, NE), lax.rem(e + 1, NE)
    halo_up = remote(hs.at[1], hr.at[0], hsem.at[0], hsem.at[1], after, t)
    halo_down = remote(hs.at[0], hr.at[1], hsem.at[2], hsem.at[3], before, t)
    halo_up.start()
    halo_down.start()

    def take_halo():
        halo_up.wait_recv()
        halo_down.wait_recv()
        for k, rs in enumerate((slice(0, 16), slice(16 + F, EXT))):
            fx[rs, :] = hr[k, :, 0:DX].astype(F32)
            fx2[rs, :] = hr[k, :, DX : 2 * DX].astype(F32)
        sx[0:16, :] = jnp.where(e == 0, -1.0, hr[0, :, 2 * DX : 2 * DX + 128].astype(F32))
        sx[16 + F : EXT, :] = jnp.where(
            e == NE - 1, -1.0, hr[1, :, 2 * DX : 2 * DX + 128].astype(F32)
        )

    def conv(ext, xs, q, backwards):
        cols = full_ds(q * 128, 128)
        kcols = full_ds(xs * DX + q * 128, 128)
        acc = jnp.zeros((F, 128), F32)
        own = sx[16 : 16 + F, :]
        for j in range(KW):
            tap = kern[KW - 1 - j if backwards else j, kcols].reshape(1, 128)
            acc += jnp.where(sx[j + 1 : j + 1 + F, :] == own, ext[j + 1 : j + 1 + F, cols] * tap, 0.0)
        return acc + ext[16 : 16 + F, cols]

    def source(first, ext, xs):
        @pl.when(c == 0)
        def _():
            if first:
                take_halo()

            @pl.loop(0, NQ)
            def _(q):
                src[:, full_ds(q * 128, 128)] = conv(ext, xs, q, False).astype(BF16)

        @pl.when(c == 1)
        def _():
            src[...] = cot[:, full_ds(xs * DX, DX)]

    def issue(part, xs, g):
        cols = full_ds(xs * DX, DX)
        slot = sub + g * F
        onehot = jnp.where((posr[0] == slot) | (posr[1] == slot), 1.0, 0.0).astype(BF16)
        sendbuf[part, g * F : g * F + F, :] = jnp.dot(
            onehot, src[...], preferred_element_type=F32
        ).astype(BF16)
        for i in range(max(8 * g, 1), 8 * g + 8):
            blk = slice(i * CAP, i * CAP + CAP)
            remote(
                sendbuf.at[part, blk, :], rows.at[c, blk, cols], asend.at[2 * part],
                arecv.at[4 * part + g], ahead(i), t,
            ).start()
        if g == 0:
            rows[c, 0:CAP, cols] = sendbuf[part, 0:CAP, :]

    source(True, fx, x)
    for g in range(4):
        issue(0, x, g)
    source(False, fx2, xo)
    for g in range(4):
        issue(1, xo, g)

    @pl.when(c == 1)
    def _():
        for i in range(1, NE):
            remote(
                gsend.at[i // 8], grecv.at[i], asend.at[1], gsem.at[0], ahead(i), t
            ).start()

    @pl.when(c == 1)
    def _():
        take_halo()

    def region(g, xs):
        return rows.at[c, g * F : g * F + F, full_ds(xs * DX, DX)]

    def to_sibling(g, xs):
        r = region(g, xs)
        remote(r, r, ssend.at[0], fs.at[g], e, sib).start()

    def arrive(part, xs, g):
        if g == 0:
            wait_recv(rows.at[c, CAP:F, full_ds(xs * DX, DX)], arecv.at[4 * part])
        else:
            wait_recv(region(g, xs), arecv.at[4 * part + g])

    def spread(g):
        arrive(0, x, g)
        r = region(g, x)
        remote(r, r, xsend.at[0], fl.at[g], e, right).start()
        remote(r, r, xsend.at[1], fr.at[g], e, left).start()
        to_sibling(g, x)

    def relay(g):
        wait_recv(region(g, xl), fl.at[g])
        to_sibling(g, xl)
        wait_recv(region(g, xr), fr.at[g])
        to_sibling(g, xr)

    def opposite(g):
        arrive(1, xo, g)
        to_sibling(g, xo)

    def from_sibling(g):
        wait_recv(rows.at[1 - c, g * F : g * F + F, :], fs.at[g])

    def weigh(g):
        parts = [jnp.broadcast_to(grecv[8 * g + q], (CAP, F)) for q in range(8)]
        w = jnp.sum(jnp.where(eye, jnp.concatenate(parts, axis=0), 0.0), axis=1, keepdims=True)
        wcol[g * F : g * F + F, :] = jnp.broadcast_to(w, (F, 128))

    def work(h):
        hr_ = slice(256 * h, 256 * h + 256)
        gacc[hr_, :] = jnp.zeros((256, 128), F32)

        @pl.loop(0, HS // 256)
        def _(n):
            cols = full_ds(n * 256, 256)
            pre = jnp.dot(rows[0, hr_, :], win[:, cols], preferred_element_type=F32)
            back = lax.dot_general(
                rows[1, hr_, :], wout[cols, :], (((1,), (1,)), ((), ())), preferred_element_type=F32
            )
            sig = jax.nn.sigmoid(pre)
            hid = (pre * sig).astype(BF16)
            hidden[hr_, cols] = hid
            prod = hid.astype(F32) * back
            gacc[hr_, :] += prod[:, 0:128] + prod[:, 128:256]
            w = wcol[hr_, 0:1]
            pgrad[hr_, cols] = (back * w * (sig * (1.0 + pre * (1.0 - sig)))).astype(BF16)

        for g in (2 * h, 2 * h + 1):
            part = jnp.sum(gacc[g * F : g * F + F, :], axis=1, keepdims=True)
            gpsend[g] = jnp.sum(
                jnp.where(eye, jnp.broadcast_to(part, (F, F)), 0.0), axis=0, keepdims=True
            )

        for tt in range(4 * h, 4 * h + 4):

            @pl.when(t == tt)
            def _():
                gpx[tt] = gpsend[tt // 2]

            @pl.when(t != tt)
            def _():
                remote(
                    gpsend.at[tt // 2], gpx.at[t], gpsem.at[0], gpsem.at[1], e, tt
                ).start()

    def gates_on():
        wait_recv(gpx.at[1 : 2 * NX], gpsem.at[1])
        gprow[0] = jnp.sum(gpx[...], axis=0)
        dz = c * (x + 1) + (1 - c) * lax.rem(NZ - x, NZ)
        zz = lax.rem(z + NZ - dz, NZ) * NY

        @pl.when(t == 0)
        def _():
            gpret[0] = gprow[0]

        @pl.when(t > 0)
        def _():
            remote(gprow.at[0], gpret.at[0], gpsem.at[2], gpsem.at[3], zz + yt[0], t).start()

        for j in range(1, NY):
            remote(
                gprow.at[0], gpret.at[j], gpsem.at[2], gpsem.at[3], zz + yt[NY - j], t
            ).start()

    def gates_home():
        @pl.when(t == 0)
        def _():
            wait_recv(gpret.at[1:NY], gpsem.at[3])

        @pl.when(t > 0)
        def _():
            wait_recv(gpret, gpsem.at[3])

        row = jnp.zeros((1, F), F32)
        for j in range(NY):
            row += jnp.where(lax.div(lane[0:1, :], CAP) == 4 * c + j, gpret[j], 0.0)
        row = jnp.broadcast_to(row, (F, F))
        for k in range(2):
            hit = jnp.where(posc[k] == lane + x * F, row, 0.0)
            col = jnp.sum(hit, axis=1, keepdims=True)
            gg[t, k : k + 1, :] = jnp.sum(
                jnp.where(eye, jnp.broadcast_to(col, (F, F)), 0.0), axis=0, keepdims=True
            )
        for i in range(1, 2 * NX):
            remote(
                gg.at[t], gg.at[t], ggsem.at[0], ggsem.at[1], e, lax.rem(t + i, 2 * NX)
            ).start()

    def scale():
        @pl.loop(0, D // 256)
        def _(n):
            cols = full_ds(n * 256, 256)
            for h in range(4):
                rh = slice(F * h, F * h + F)
                scaled[rh, cols] = (wcol[rh, 0:1] * rows[1, rh, cols].astype(F32)).astype(BF16)

    def inputs_grad(h):
        rh = slice(256 * h, 256 * h + 256)

        for k, xs in enumerate((xo, xr, xl, x)):
            cols = full_ds(xs * DX, DX)
            ip[rh, cols] = lax.dot_general(
                pgrad[rh, :], win[cols, :], (((1,), (1,)), ((), ())), preferred_element_type=F32
            ).astype(BF16)
            for g in (2 * h, 2 * h + 1):
                other = pl.ds(pl.multiple_of(F * g + (1 - c) * HF, HF), HF)
                arrived = sibsem.at[(1 if k == 0 else 5) + g]
                remote(
                    ip.at[other, cols], sibrecv.at[g, :, cols], sibsem.at[0], arrived, e, sib
                ).start()

    def ring1(h):
        oc = full_ds(xo * DX, DX)
        wait_recv(sibrecv.at[h, :, oc], sibsem.at[1 + h])
        own = pl.ds(pl.multiple_of(F * h + c * HF, HF), HF)
        cs[h, :, oc] = (ip[own, oc].astype(F32) + sibrecv[h, :, oc].astype(F32)).astype(BF16)
        remote(cs.at[h, 0:32, oc], r1.at[h, 0], rsem.at[0], rsem.at[4 + h], e, right).start()
        remote(cs.at[h, 32:64, oc], r1.at[h, 1], rsem.at[1], rsem.at[8 + h], e, left).start()

        wait_recv(sibrecv.at[h, :, 0 : 3 * DX], sibsem.at[5 + h])
        for xs in (xr, xl, x):
            cols = full_ds(xs * DX, DX)
            cs[h, :, cols] = (
                ip[own, cols].astype(F32) + sibrecv[h, :, cols].astype(F32)
            ).astype(BF16)

    def ring2(h):
        wait_recv(r1.at[h, 0], rsem.at[4 + h])
        rc = full_ds(xr * DX, DX)
        s2[h, 0, 0:32, :] = (cs[h, 0:32, rc].astype(F32) + r1[h, 0].astype(F32)).astype(BF16)
        s2[h, 0, 32:64, :] = cs[h, 32:64, rc]
        remote(s2.at[h, 0], r2.at[h, 0], rsem.at[2], rsem.at[12 + h], e, right).start()
        wait_recv(r1.at[h, 1], rsem.at[8 + h])
        lc = full_ds(xl * DX, DX)
        s2[h, 1, 32:64, :] = (cs[h, 32:64, lc].astype(F32) + r1[h, 1].astype(F32)).astype(BF16)
        s2[h, 1, 0:32, :] = cs[h, 0:32, lc]
        remote(s2.at[h, 1], r2.at[h, 1], rsem.at[3], rsem.at[16 + h], e, left).start()

    def ring3(h):
        wait_recv(r2.at[h, 0], rsem.at[12 + h])
        wait_recv(r2.at[h, 1], rsem.at[16 + h])
        fin[h] = (
            cs[h, :, xcols].astype(F32) + r2[h, 0].astype(F32) + r2[h, 1].astype(F32)
        ).astype(BF16)

        for q in range(4):
            blk = slice(q * CAP, q * CAP + CAP)
            i = 8 * h + q

            def send():
                to = jnp.where(c == 0, behind(i), behind(i + 4))
                place = pl.ds(pl.multiple_of(i * CAP + c * HF, CAP), CAP)
                for tt in (t, sib):
                    remote(
                        fin.at[h, blk, :], ret.at[place, :], retsem.at[0], retsem.at[1], to, tt
                    ).start()

            if i == 0:

                @pl.when(c == 0)
                def _():
                    ret[0:CAP, :] = fin[0, 0:CAP, :]
                    remote(
                        fin.at[h, blk, :], ret.at[0:CAP, :], retsem.at[0], retsem.at[1], e, sib
                    ).start()

                pl.when(c == 1)(send)
            else:
                send()

    def first_grad(lo, hi):
        @pl.loop(lo, hi)
        def _(m):
            cols = full_ds(m * 256, 256)
            wig[cols, :] = lax.dot_general(
                rows[0, :, cols], pgrad[...], (((0,), (0,)), ((), ())), preferred_element_type=F32
            ).astype(BF16)

    def second_grad(lo, hi):
        @pl.loop(lo, hi)
        def _(m):
            cols = full_ds(m * 256, 256)
            for n in range(2):
                nc = slice(n * 768, n * 768 + 768)
                wog[cols, nc] = lax.dot_general(
                    hidden[:, cols], scaled[:, nc], (((0,), (0,)), ((), ())),
                    preferred_element_type=F32,
                ).astype(BF16)

    spread(0)
    spread(1)
    spread(2)
    spread(3)
    opposite(0)
    relay(0)
    opposite(1)

    share = remote(grecv, grecv, gsem.at[1], gsem.at[2], e, sib)

    @pl.when(c == 1)
    def _():
        wait_recv(grecv.at[1:NE], gsem.at[0])
        share.start()

    relay(1)

    @pl.when(c == 0)
    def _():
        share.wait_recv()

    for g in range(4):
        weigh(g)
    for load in loads[6:]:
        load.wait()
    from_sibling(0)
    from_sibling(1)
    work(0)
    opposite(2)
    relay(2)
    opposite(3)
    relay(3)
    inputs_grad(0)
    from_sibling(2)
    from_sibling(3)
    ring1(0)
    ring1(1)
    work(1)
    ring2(0)
    ring2(1)
    inputs_grad(1)
    ring1(2)
    ring1(3)
    ring3(0)
    ring3(1)
    ring2(2)
    ring2(3)
    gates_on()
    first_grad(0, 2)
    ring3(2)
    ring3(3)
    first_grad(2, 6)
    scale()
    second_grad(0, 3)

    @pl.when(c == 0)
    def _():
        wait_recv(ret.at[CAP:SLOTS, :], retsem.at[1])

    @pl.when(c == 1)
    def _():
        wait_recv(ret, retsem.at[1])

    mg = cot[:, xcols].astype(F32)
    for g in range(4):
        slot = lane + g * F
        pick = jnp.where((posc[0] == slot) | (posc[1] == slot), 1.0, 0.0).astype(BF16)
        mg += jnp.dot(pick, ret[g * F : g * F + F, :], preferred_element_type=F32)
    mgx[16 : 16 + F, :] = mg

    def gather_own(r, sem):
        remote(r, r, sem.at[0], sem.at[3], e, facing).start()
        remote(r, r, sem.at[0], sem.at[1], e, right).start()
        remote(r, r, sem.at[0], sem.at[2], e, left).start()
        remote(r, r, sem.at[4], sem.at[5], e, sib).start()

    def gather_rest(view, sem):
        for k, xs in ((1, xl), (2, xr), (3, xo)):
            r = view(xs)
            wait_recv(r, sem.at[k])
            remote(r, r, sem.at[4], sem.at[5], e, sib).start()

    @pl.when(c == 0)
    def _():
        up = remote(
            mgx.at[F : F + 16, :], mgx.at[0:16, :], mhsem.at[0], mhsem.at[1], after, t
        )
        down = remote(
            mgx.at[16:32, :], mgx.at[16 + F : EXT, :], mhsem.at[2], mhsem.at[3], before, t
        )
        up.start()
        down.start()
        gates_home()
        up.wait_recv()
        down.wait_recv()

        for q in range(NQ):
            tile = full_ds(x * DX + q * 128, 128)
            fgall[:, tile] = conv(mgx, x, q, True).astype(BF16)
            gather_own(fgall.at[:, tile], fgsem)
        gather_rest(lambda xs: fgall.at[:, full_ds(xs * DX, DX)], fgsem)
        for k, xs in ((0, x), (1, xl), (2, xr), (3, xo)):
            wait_recv(kfull.at[xs], kfsem.at[k])
        wait_send(fgall.at[:, 0 : 3 * DX], fgsem.at[0])
        wait_send(fgall, fgsem.at[4])
        up.wait_send()
        down.wait_send()

    @pl.when(c == 1)
    def _():
        kg[...] = jnp.zeros_like(kg)
        for j in range(NE):
            if j < KW:
                near = sx[j + 1 : j + 1 + F, :] == sx[16 : 16 + F, :]
                for q in range(NQ):
                    cols = slice(q * 128, q * 128 + 128)
                    prod = jnp.where(
                        near, fx[j + 1 : j + 1 + F, cols] * mgx[16 : 16 + F, cols], 0.0
                    )
                    kg[j, q : q + 1, :] = jnp.sum(prod, axis=0, keepdims=True)

            if j % 8 == 7:

                @pl.when(y != j // 8)
                def _():
                    remote(
                        kg.at[j - 7 : j + 1], krecv.at[y], ksem.at[0], ksem.at[1],
                        z * NY + j // 8, t,
                    ).start()

                @pl.when(y == j // 8)
                def _():
                    krecv[y] = kg[j - 7 : j + 1]

        gates_home()
        wait_recv(krecv.at[1:NY], ksem.at[1])
        kz[z] = jnp.sum(krecv[...], axis=0)
        for k in range(1, NZ):
            remote(kz.at[z], kz.at[z], ksem.at[2], ksem.at[3], zt[k] + y, t).start()
        wait_recv(kz.at[1:NZ], ksem.at[3])
        own = pl.ds(pl.multiple_of(y * 8, 8), 8)
        kfull[x, own] = jnp.sum(kz[...], axis=0)
        mine = kfull.at[x, own]
        for k, xs in ((3, xo), (1, xr), (2, xl), (0, x)):
            for m in range(NY):
                for cc in (0, 1):
                    if k == 0 and m == 0 and cc == 1:
                        continue
                    remote(
                        mine, mine, kfsem.at[4], kfsem.at[k], z * NY + yt[m], 2 * xs + cc
                    ).start()
        wait_recv(kfull.at[x, 0:24], kfsem.at[0])
        for k, xs in ((1, xl), (2, xr), (3, xo)):
            wait_recv(kfull.at[xs], kfsem.at[k])
        wait_recv(fgall, fgsem.at[5])
        wait_send(krecv.at[1:NY], ksem.at[0])
        wait_send(kz.at[1:NZ], ksem.at[2])
        wait_send(ip.at[0:496, 0:512], kfsem.at[4])

    wait_recv(gg.at[1 : 2 * NX], ggsem.at[1])
    gg_out[...] = jnp.sum(gg[...], axis=0)
    fg_out[...] = fgall[...]
    for xs in range(NX):
        for q in range(NQ):
            kg_out[:, xs * DX + q * 128 : xs * DX + q * 128 + 128] = kfull[xs, 0:KW, q, :]

    halo_up.wait_send()
    halo_down.wait_send()
    wait_send(sendbuf.at[0, CAP:SLOTS, :], asend.at[0])
    wait_send(sendbuf.at[1, CAP:SLOTS, :], asend.at[2])

    @pl.when(c == 1)
    def _():
        wait_send(grecv.at[1:NE], asend.at[1])
        share.wait_send()

    wait_send(rows.at[c, :, xcols], xsend.at[0])
    wait_send(rows.at[c, :, xcols], xsend.at[1])
    wait_send(rows.at[c], ssend.at[0])
    wait_send(gpx.at[1 : 2 * NX], gpsem.at[0])

    @pl.when(t == 0)
    def _():
        wait_send(gpret.at[1:NY], gpsem.at[2])

    @pl.when(t > 0)
    def _():
        wait_send(gpret, gpsem.at[2])

    wait_send(sibrecv, sibsem.at[0])
    wait_send(r1.at[:, 0], rsem.at[0])
    wait_send(r1.at[:, 1], rsem.at[1])
    wait_send(s2.at[:, 0], rsem.at[2])
    wait_send(s2.at[:, 1], rsem.at[3])

    @pl.when(c == 0)
    def _():
        wait_send(ip.at[CAP:SLOTS, 0:DX], retsem.at[0])

    @pl.when(c == 1)
    def _():
        wait_send(ip.at[:, 0:DX], retsem.at[0])

    wait_send(gg.at[1 : 2 * NX], ggsem.at[0])


def write_out(*refs):
    copies = [pltpu.make_async_copy(refs[k], refs[5 + k], refs[10].at[k]) for k in range(5)]
    for copy in copies:
        copy.start()
    for copy in copies:
        copy.wait()


def on_device(frames, cotangent, segment_ids, kernel, expert_ids, gates, w_in, w_out):
    vmem = pl.BlockSpec(memory_space=pltpu.VMEM)
    hbm = pl.BlockSpec(memory_space=pltpu.HBM)
    dma = pltpu.SemaphoreType.DMA
    V = pltpu.VMEM
    scratch = dict(
        frames=V((F, D), BF16),
        cot=V((F, D), BF16),
        seg=V((1, F), jnp.int32),
        kern=V((KW, D), F32),
        ids=V((2, F), jnp.int32),
        gates=V((2, F), BF16),
        win=V((D, HS), BF16),
        wout=V((HS, D), BF16),
        rows=V((2, SLOTS, D), BF16),
        sendbuf=V((2, SLOTS, DX), BF16),
        src=V((F, DX), BF16),
        hs=V((2, 16, 2 * DX + 128), BF16),
        hr=V((2, 16, 2 * DX + 128), BF16),
        fx=V((EXT, DX), F32),
        fx2=V((EXT, DX), F32),
        sx=V((EXT, 128), F32),
        gsend=V((4, 1, 128), F32),
        grecv=V((NE, 1, 128), F32),
        wcol=V((SLOTS, 128), F32),
        scaled=V((SLOTS, D), BF16),
        hidden=V((SLOTS, HS), BF16),
        pgrad=V((SLOTS, HS), BF16),
        gacc=V((SLOTS, 128), F32),
        gpsend=V((4, 1, 128), F32),
        gpx=V((2 * NX, 1, 128), F32),
        gprow=V((1, 1, 128), F32),
        gpret=V((NY, 1, 128), F32),
        ip=V((SLOTS, D), BF16),
        sibrecv=V((4, HF, D), BF16),
        cs=V((4, HF, D), BF16),
        r1=V((4, 2, HF // 2, DX), BF16),
        s2=V((4, 2, HF, DX), BF16),
        r2=V((4, 2, HF, DX), BF16),
        fin=V((4, HF, DX), BF16),
        ret=V((SLOTS, DX), BF16),
        mgx=V((EXT, DX), F32),
        fgall=V((F, D), BF16),
        kg=V((NE, 4, 128), F32),
        krecv=V((NY, 8, 4, 128), F32),
        kz=V((NZ, 8, 4, 128), F32),
        kfull=V((NX, NE, 4, 128), F32),
        gg=V((2 * NX, 2, 128), F32),
        posr=V((2, F, F), jnp.int32),
        posc=V((2, F, F), jnp.int32),
        lsem=dma((8,)),
        hsem=dma((4,)),
        asend=dma((3,)),
        arecv=dma((8,)),
        gsem=dma((3,)),
        xsend=dma((2,)),
        ssend=dma((1,)),
        fl=dma((4,)),
        fr=dma((4,)),
        fs=dma((4,)),
        gpsem=dma((4,)),
        sibsem=dma((9,)),
        rsem=dma((20,)),
        retsem=dma((2,)),
        mhsem=dma((4,)),
        fgsem=dma((6,)),
        ksem=dma((4,)),
        kfsem=dma((5,)),
        ggsem=dma((2,)),
    )
    made = pl.pallas_call(
        body,
        out_shape=(
            V((F, D), BF16),
            V((KW, D), F32),
            V((D, HS), BF16),
            V((HS, D), BF16),
            V((2, F), F32),
        ),
        in_specs=[hbm] * 8,
        out_specs=(vmem,) * 5,
        scratch_shapes=list(scratch.values()),
        compiler_params=pltpu.CompilerParams(
            collective_id=0, has_side_effects=True, vmem_limit_bytes=56 * 1024 * 1024
        ),
    )(
        frames,
        cotangent,
        segment_ids.reshape(1, F),
        kernel,
        expert_ids.T,
        gates.T,
        w_in[0],
        w_out[0],
    )
    fg, kg, wig, wog, gg = pl.pallas_call(
        write_out,
        out_shape=tuple(pltpu.HBM(v.shape, v.dtype) for v in made),
        in_specs=[vmem] * 5,
        out_specs=(hbm,) * 5,
        scratch_shapes=[dma((5,))],
        compiler_params=pltpu.CompilerParams(vmem_limit_bytes=2 * 1024 * 1024),
    )(*made)
    return fg, kg, wig[None], wog[None], gg.T


def solution(mesh):
    return jax.shard_map(
        on_device,
        mesh=mesh,
        in_specs=(
            P("expert", None),
            P("expert", None),
            P("expert"),
            P(),
            P("expert", None),
            P("expert", None),
            P("expert", None, "tensor"),
            P("expert", "tensor", None),
        ),
        out_specs=(
            P("expert", None),
            P(),
            P("expert", None, "tensor"),
            P("expert", "tensor", None),
            P("expert", None),
        ),
        check_vma=False,
    )
```

```python
import jax
import jax.numpy as jnp
from jax import lax
from jax.experimental import pallas as pl
from jax.experimental.pallas import tpu as pltpu
from jax.sharding import PartitionSpec as P

MESH = pl.DeviceIdType.MESH
F32 = jnp.float32
BF16 = jnp.bfloat16
NZ, NY, NX = 8, 4, 4
NE = NZ * NY
F = 128
HF = F // 2
D = 1536
HS = 768
KW = 31
CAP = 16
SLOTS = NE * CAP
DX = D // NX
NQ = DX // 128
EXT = F + 32


def full_ds(start, size):
    return pl.ds(pl.multiple_of(start, 128), size)


def body(
    frames_in, cot_in, seg_in, kern_in, ids_in, gates_in, w_in, w_out,
    fg_out, kg_out, wig, wog, gg_out,
    frames, cot, seg, kern, ids, gates,
    win, wout, rows, sendbuf, src, hs, hr, fx, fx2, sx, gsend, grecv, wcol,
    scaled, hidden, pgrad, gacc, gpsend, gpx, gprow, gpret, ip, sibrecv, cs, r1, s2, r2, fin, ret,
    mgx, fgall, kg, krecv, kz, kfull, gg, posr, posc,
    lsem, hsem, asend, arecv, gsem, xsend, ssend, fl, fr, fs, gpsem, sibsem, rsem,
    retsem, mhsem, fgsem, ksem, kfsem, ggsem,
):
    e = lax.axis_index("expert")
    t = lax.axis_index("tensor")
    z, y = lax.div(e, NY), lax.rem(e, NY)
    x, c = lax.div(t, 2), lax.rem(t, 2)
    sib = t + 1 - 2 * c
    xr, xl, xo = lax.rem(x + 1, NX), lax.rem(x + 3, NX), lax.rem(x + 2, NX)
    right, left, facing = xr * 2 + c, xl * 2 + c, xo * 2 + c
    xcols = full_ds(x * DX, DX)

    zt = [lax.rem(z + k, NZ) * NY for k in range(NZ)]
    yt = [lax.rem(y + k, NY) for k in range(NY)]

    def offset(i):
        p = i // NY
        return ((p + 1) // 2 if p % 2 else (NZ - p // 2) % NZ), i % NY

    def ahead(i):
        dz, dy = offset(i)
        return zt[dz] + yt[dy]

    def behind(i):
        dz, dy = offset(i)
        return zt[(NZ - dz) % NZ] + yt[(NY - dy) % NY]

    def remote(s, d, ss, rs, ee, tt):
        return pltpu.make_async_remote_copy(
            src_ref=s, dst_ref=d, send_sem=ss, recv_sem=rs, device_id=(ee, tt), device_id_type=MESH
        )

    def wait_recv(ref, sem):
        remote(ref, ref, sem, sem, e, sib).wait_recv()

    def wait_send(ref, sem):
        remote(ref, ref, sem, sem, e, sib).wait_send()

    barrier = pltpu.get_barrier_semaphore()

    for i in range(1, NE):
        for tt in (t, sib):
            pl.semaphore_signal(barrier, inc=1, device_id=(ahead(i), tt), device_id_type=MESH)
    for i in range(1, 2 * NX):
        pl.semaphore_signal(
            barrier, inc=1, device_id=(e, lax.rem(t + i, 2 * NX)), device_id_type=MESH
        )
    for tt in (right, left, facing, right + sib - t, left + sib - t, facing + sib - t):
        for m in range(1, NY):
            pl.semaphore_signal(
                barrier, inc=1, device_id=(z * NY + yt[m], tt), device_id_type=MESH
            )
    pairs = (
        (ids_in, ids), (gates_in, gates), (seg_in, seg), (frames_in, frames), (cot_in, cot),
        (kern_in, kern), (w_in, win), (w_out, wout),
    )
    loads = [pltpu.make_async_copy(a, b, lsem.at[k]) for k, (a, b) in enumerate(pairs)]
    for load in loads:
        load.start()
    for load in loads[:3]:
        load.wait()

    lane = lax.broadcasted_iota(jnp.int32, (F, F), 1)
    sub = lax.broadcasted_iota(jnp.int32, (F, F), 0)
    eye = lane == sub
    idr = [jnp.broadcast_to(ids[k : k + 1, :], (F, F)).astype(F32) for k in range(2)]
    idc = [v.T for v in idr]

    def place(idf, rank):
        idv = idf.astype(jnp.int32)
        dz = (idv // NY - z + NZ) & (NZ - 1)
        dy = (idv - (idv // NY) * NY - y + NY) & (NY - 1)
        p = jnp.maximum(jnp.where(dz <= NZ // 2, 2 * dz - 1, 2 * NZ - 2 * dz), 0)
        return (p * NY + dy) * CAP + rank.astype(jnp.int32)

    for k in range(2):
        hits = jnp.where(idc[0] == idr[k], 1.0, 0.0) + jnp.where(idc[1] == idr[k], 1.0, 0.0)
        rank = jnp.sum(jnp.where(sub < lane, hits, 0.0), axis=0, keepdims=True)
        posr[k] = place(idr[k], jnp.broadcast_to(rank, (F, F)))
        hits = jnp.where(idr[0] == idc[k], 1.0, 0.0) + jnp.where(idr[1] == idc[k], 1.0, 0.0)
        rank = jnp.sum(jnp.where(lane < sub, hits, 0.0), axis=1, keepdims=True)
        posc[k] = place(idc[k], jnp.broadcast_to(rank, (F, F)))

    for g in range(4):
        total = jnp.zeros((1, F), F32)
        for k in range(2):
            gcol = jnp.broadcast_to(gates[k : k + 1, :].astype(F32), (F, F)).T
            total += jnp.sum(
                jnp.where(posc[k] == lane + g * F, gcol, 0.0), axis=0, keepdims=True
            )
        gsend[g] = total

    @pl.when(c == 1)
    def _():
        grecv[0] = gsend[0]

    for load in loads[3:6]:
        load.wait()
    segr = jnp.broadcast_to(seg[...], (F, F)).astype(F32)
    segc = segr.T
    sx[16 : 16 + F, :] = segc
    ocols = full_ds(xo * DX, DX)
    for k, rs in enumerate((slice(0, 16), slice(F - 16, F))):
        hs[k, :, 0:DX] = frames[rs, xcols]
        hs[k, :, DX : 2 * DX] = frames[rs, ocols]
        hs[k, :, 2 * DX : 2 * DX + 128] = segc[rs].astype(BF16)

    @pl.loop(0, NQ)
    def _(q):
        tile = full_ds(q * 128, 128)
        fx[16 : 16 + F, tile] = frames[:, full_ds(x * DX + q * 128, 128)].astype(F32)
        fx2[16 : 16 + F, tile] = frames[:, full_ds(xo * DX + q * 128, 128)].astype(F32)

    def conv(ext, xs, q, backwards, lo, n):
        cols = full_ds(q * 128, 128)
        kcols = full_ds(xs * DX + q * 128, 128)
        acc = ext[16 + lo : 16 + lo + n, cols]
        own = sx[16 + lo : 16 + lo + n, :]
        for j in range(KW):
            tap = kern[KW - 1 - j if backwards else j, kcols].reshape(1, 128)
            near = slice(j + 1 + lo, j + 1 + lo + n)
            acc += jnp.where(sx[near, :] == own, ext[near, cols] * tap, 0.0)
        return acc

    @pl.when(c == 0)
    def _():
        for part, (ext, xs) in enumerate(((fx, x), (fx2, xo))):

            @pl.loop(0, NQ)
            def _(q):
                src[part, 16 : F - 16, full_ds(q * 128, 128)] = conv(
                    ext, xs, q, False, 16, F - 32
                ).astype(BF16)

    @pl.when(c == 1)
    def _():
        src[0] = cot[:, xcols]
        src[1] = cot[:, ocols]

    pl.semaphore_wait(barrier, 2 * (NE - 1) + 2 * NX - 1 + 6 * (NY - 1))

    before, after = lax.rem(e + NE - 1, NE), lax.rem(e + 1, NE)
    halo_up = remote(hs.at[1], hr.at[0], hsem.at[0], hsem.at[1], after, t)
    halo_down = remote(hs.at[0], hr.at[1], hsem.at[2], hsem.at[3], before, t)
    halo_up.start()
    halo_down.start()

    def take_halo():
        halo_up.wait_recv()
        halo_down.wait_recv()
        for k, rs in enumerate((slice(0, 16), slice(16 + F, EXT))):
            fx[rs, :] = hr[k, :, 0:DX].astype(F32)
            fx2[rs, :] = hr[k, :, DX : 2 * DX].astype(F32)
        sx[0:16, :] = jnp.where(e == 0, -1.0, hr[0, :, 2 * DX : 2 * DX + 128].astype(F32))
        sx[16 + F : EXT, :] = jnp.where(
            e == NE - 1, -1.0, hr[1, :, 2 * DX : 2 * DX + 128].astype(F32)
        )

    def source(part, ext, xs):
        @pl.when(c == 0)
        def _():
            if part == 0:
                take_halo()

            @pl.loop(0, NQ)
            def _(q):
                cols = full_ds(q * 128, 128)
                for lo in (0, F - 16):
                    src[part, lo : lo + 16, cols] = conv(ext, xs, q, False, lo, 16).astype(BF16)

    def issue(part, xs, g):
        cols = full_ds(xs * DX, DX)
        slot = sub + g * F
        onehot = jnp.where((posr[0] == slot) | (posr[1] == slot), 1.0, 0.0).astype(BF16)
        sendbuf[part, g * F : g * F + F, :] = jnp.dot(
            onehot, src[part], preferred_element_type=F32
        ).astype(BF16)
        for i in range(max(8 * g, 1), 8 * g + 8):
            blk = slice(i * CAP, i * CAP + CAP)
            remote(
                sendbuf.at[part, blk, :], rows.at[c, blk, cols], asend.at[2 * part],
                arecv.at[4 * part + g], ahead(i), t,
            ).start()
        if g == 0:
            rows[c, 0:CAP, cols] = sendbuf[part, 0:CAP, :]

    source(0, fx, x)
    for g in range(4):
        issue(0, x, g)
    @pl.when(c == 1)
    def _():
        take_halo()

    def region(g, xs):
        return rows.at[c, g * F : g * F + F, full_ds(xs * DX, DX)]

    def to_sibling(g, xs):
        r = region(g, xs)
        remote(r, r, ssend.at[0], fs.at[g], e, sib).start()

    def arrive(part, xs, g):
        if g == 0:
            wait_recv(rows.at[c, CAP:F, full_ds(xs * DX, DX)], arecv.at[4 * part])
        else:
            wait_recv(region(g, xs), arecv.at[4 * part + g])

    def spread(g):
        arrive(0, x, g)
        r = region(g, x)
        remote(r, r, xsend.at[0], fl.at[g], e, right).start()
        remote(r, r, xsend.at[1], fr.at[g], e, left).start()
        to_sibling(g, x)

    def relay(g):
        wait_recv(region(g, xl), fl.at[g])
        to_sibling(g, xl)
        wait_recv(region(g, xr), fr.at[g])
        to_sibling(g, xr)

    def opposite(g):
        arrive(1, xo, g)
        to_sibling(g, xo)

    def from_sibling(g):
        wait_recv(rows.at[1 - c, g * F : g * F + F, :], fs.at[g])

    def weigh(g):
        parts = [jnp.broadcast_to(grecv[8 * g + q], (CAP, F)) for q in range(8)]
        w = jnp.sum(jnp.where(eye, jnp.concatenate(parts, axis=0), 0.0), axis=1, keepdims=True)
        wcol[g * F : g * F + F, :] = jnp.broadcast_to(w, (F, 128))

    def work(h):
        hr_ = slice(256 * h, 256 * h + 256)
        gacc[hr_, :] = jnp.zeros((256, 128), F32)

        @pl.loop(0, HS // 256)
        def _(n):
            cols = full_ds(n * 256, 256)
            pre = jnp.dot(rows[0, hr_, :], win[:, cols], preferred_element_type=F32)
            back = lax.dot_general(
                rows[1, hr_, :], wout[cols, :], (((1,), (1,)), ((), ())), preferred_element_type=F32
            )
            sig = jax.nn.sigmoid(pre)
            hid = (pre * sig).astype(BF16)
            hidden[hr_, cols] = hid
            prod = hid.astype(F32) * back
            gacc[hr_, :] += prod[:, 0:128] + prod[:, 128:256]
            w = wcol[hr_, 0:1]
            pgrad[hr_, cols] = (back * w * (sig * (1.0 + pre * (1.0 - sig)))).astype(BF16)

        for g in (2 * h, 2 * h + 1):
            part = jnp.sum(gacc[g * F : g * F + F, :], axis=1, keepdims=True)
            gpsend[g] = jnp.sum(
                jnp.where(eye, jnp.broadcast_to(part, (F, F)), 0.0), axis=0, keepdims=True
            )

        for tt in range(4 * h, 4 * h + 4):

            @pl.when(t == tt)
            def _():
                gpx[tt] = gpsend[tt // 2]

            @pl.when(t != tt)
            def _():
                remote(
                    gpsend.at[tt // 2], gpx.at[t], gpsem.at[0], gpsem.at[1], e, tt
                ).start()

    def gates_on():
        wait_recv(gpx.at[1 : 2 * NX], gpsem.at[1])
        gprow[0] = jnp.sum(gpx[...], axis=0)
        dz = c * (x + 1) + (1 - c) * lax.rem(NZ - x, NZ)
        zz = lax.rem(z + NZ - dz, NZ) * NY

        @pl.when(t == 0)
        def _():
            gpret[0] = gprow[0]

        @pl.when(t > 0)
        def _():
            remote(gprow.at[0], gpret.at[0], gpsem.at[2], gpsem.at[3], zz + yt[0], t).start()

        for j in range(1, NY):
            remote(
                gprow.at[0], gpret.at[j], gpsem.at[2], gpsem.at[3], zz + yt[NY - j], t
            ).start()

    def gates_home():
        @pl.when(t == 0)
        def _():
            wait_recv(gpret.at[1:NY], gpsem.at[3])

        @pl.when(t > 0)
        def _():
            wait_recv(gpret, gpsem.at[3])

        row = jnp.zeros((1, F), F32)
        for j in range(NY):
            row += jnp.where(lax.div(lane[0:1, :], CAP) == 4 * c + j, gpret[j], 0.0)
        row = jnp.broadcast_to(row, (F, F))
        for k in range(2):
            hit = jnp.where(posc[k] == lane + x * F, row, 0.0)
            col = jnp.sum(hit, axis=1, keepdims=True)
            gg[t, k : k + 1, :] = jnp.sum(
                jnp.where(eye, jnp.broadcast_to(col, (F, F)), 0.0), axis=0, keepdims=True
            )
        for i in range(1, 2 * NX):
            remote(
                gg.at[t], gg.at[t], ggsem.at[0], ggsem.at[1], e, lax.rem(t + i, 2 * NX)
            ).start()

    def scale():
        @pl.loop(0, D // 256)
        def _(n):
            cols = full_ds(n * 256, 256)
            for h in range(4):
                rh = slice(F * h, F * h + F)
                scaled[rh, cols] = (wcol[rh, 0:1] * rows[1, rh, cols].astype(F32)).astype(BF16)

    def inputs_grad(h):
        rh = slice(256 * h, 256 * h + 256)

        for k, xs in enumerate((xo, xr, xl, x)):
            cols = full_ds(xs * DX, DX)
            ip[rh, cols] = lax.dot_general(
                pgrad[rh, :], win[cols, :], (((1,), (1,)), ((), ())), preferred_element_type=F32
            ).astype(BF16)
            for g in (2 * h, 2 * h + 1):
                other = pl.ds(pl.multiple_of(F * g + (1 - c) * HF, HF), HF)
                arrived = sibsem.at[(1 if k == 0 else 5) + g]
                remote(
                    ip.at[other, cols], sibrecv.at[g, :, cols], sibsem.at[0], arrived, e, sib
                ).start()

    def ring1(h):
        oc = full_ds(xo * DX, DX)
        wait_recv(sibrecv.at[h, :, oc], sibsem.at[1 + h])
        own = pl.ds(pl.multiple_of(F * h + c * HF, HF), HF)
        cs[h, :, oc] = (ip[own, oc].astype(F32) + sibrecv[h, :, oc].astype(F32)).astype(BF16)
        remote(cs.at[h, 0:32, oc], r1.at[h, 0], rsem.at[0], rsem.at[4 + h], e, right).start()
        remote(cs.at[h, 32:64, oc], r1.at[h, 1], rsem.at[1], rsem.at[8 + h], e, left).start()

        wait_recv(sibrecv.at[h, :, 0 : 3 * DX], sibsem.at[5 + h])
        for xs in (xr, xl, x):
            cols = full_ds(xs * DX, DX)
            cs[h, :, cols] = (
                ip[own, cols].astype(F32) + sibrecv[h, :, cols].astype(F32)
            ).astype(BF16)

    def ring2(h):
        wait_recv(r1.at[h, 0], rsem.at[4 + h])
        rc = full_ds(xr * DX, DX)
        s2[h, 0, 0:32, :] = (cs[h, 0:32, rc].astype(F32) + r1[h, 0].astype(F32)).astype(BF16)
        s2[h, 0, 32:64, :] = cs[h, 32:64, rc]
        remote(s2.at[h, 0], r2.at[h, 0], rsem.at[2], rsem.at[12 + h], e, right).start()
        wait_recv(r1.at[h, 1], rsem.at[8 + h])
        lc = full_ds(xl * DX, DX)
        s2[h, 1, 32:64, :] = (cs[h, 32:64, lc].astype(F32) + r1[h, 1].astype(F32)).astype(BF16)
        s2[h, 1, 0:32, :] = cs[h, 0:32, lc]
        remote(s2.at[h, 1], r2.at[h, 1], rsem.at[3], rsem.at[16 + h], e, left).start()

    def ring3(h):
        wait_recv(r2.at[h, 0], rsem.at[12 + h])
        wait_recv(r2.at[h, 1], rsem.at[16 + h])
        fin[h] = (
            cs[h, :, xcols].astype(F32) + r2[h, 0].astype(F32) + r2[h, 1].astype(F32)
        ).astype(BF16)

        for q in range(4):
            blk = slice(q * CAP, q * CAP + CAP)
            i = 8 * h + q

            def send():
                to = jnp.where(c == 0, behind(i), behind(i + 4))
                place = pl.ds(pl.multiple_of(i * CAP + c * HF, CAP), CAP)
                for tt in (t, sib):
                    remote(
                        fin.at[h, blk, :], ret.at[place, :], retsem.at[0], retsem.at[1], to, tt
                    ).start()

            if i == 0:

                @pl.when(c == 0)
                def _():
                    ret[0:CAP, :] = fin[0, 0:CAP, :]
                    remote(
                        fin.at[h, blk, :], ret.at[0:CAP, :], retsem.at[0], retsem.at[1], e, sib
                    ).start()

                pl.when(c == 1)(send)
            else:
                send()

    def first_grad(lo, hi):
        @pl.loop(lo, hi)
        def _(m):
            cols = full_ds(m * 256, 256)
            wig[cols, :] = lax.dot_general(
                rows[0, :, cols], pgrad[...], (((0,), (0,)), ((), ())), preferred_element_type=F32
            ).astype(BF16)

    def second_grad(lo, hi):
        @pl.loop(lo, hi)
        def _(m):
            cols = full_ds(m * 256, 256)
            for n in range(2):
                nc = slice(n * 768, n * 768 + 768)
                wog[cols, nc] = lax.dot_general(
                    hidden[:, cols], scaled[:, nc], (((0,), (0,)), ((), ())),
                    preferred_element_type=F32,
                ).astype(BF16)

    source(1, fx2, xo)
    issue(1, xo, 0)
    issue(1, xo, 1)
    spread(0)
    issue(1, xo, 2)
    issue(1, xo, 3)
    spread(1)

    @pl.when(c == 1)
    def _():
        for i in range(1, NE):
            remote(
                gsend.at[i // 8], grecv.at[i], asend.at[1], gsem.at[0], ahead(i), t
            ).start()

    spread(2)
    spread(3)
    opposite(0)
    relay(0)
    opposite(1)

    share = remote(grecv, grecv, gsem.at[1], gsem.at[2], e, sib)

    @pl.when(c == 1)
    def _():
        wait_recv(grecv.at[1:NE], gsem.at[0])
        share.start()

    relay(1)

    @pl.when(c == 0)
    def _():
        share.wait_recv()

    for g in range(4):
        weigh(g)
    for load in loads[6:]:
        load.wait()
    from_sibling(0)
    from_sibling(1)
    work(0)
    opposite(2)
    relay(2)
    opposite(3)
    relay(3)
    inputs_grad(0)
    from_sibling(2)
    from_sibling(3)
    ring1(0)
    ring1(1)
    work(1)
    ring2(0)
    ring2(1)
    inputs_grad(1)
    ring1(2)
    ring1(3)
    ring3(0)
    ring3(1)
    ring2(2)
    ring2(3)
    gates_on()
    first_grad(0, 2)
    ring3(2)
    ring3(3)
    first_grad(2, 6)
    scale()
    second_grad(0, 3)

    @pl.when(c == 0)
    def _():
        wait_recv(ret.at[CAP:SLOTS, :], retsem.at[1])

    @pl.when(c == 1)
    def _():
        wait_recv(ret, retsem.at[1])

    mg = cot[:, xcols].astype(F32)
    for g in range(4):
        slot = lane + g * F
        pick = jnp.where((posc[0] == slot) | (posc[1] == slot), 1.0, 0.0).astype(BF16)
        mg += jnp.dot(pick, ret[g * F : g * F + F, :], preferred_element_type=F32)
    mgx[16 : 16 + F, :] = mg

    def gather_own(r, sem):
        remote(r, r, sem.at[0], sem.at[3], e, facing).start()
        remote(r, r, sem.at[0], sem.at[1], e, right).start()
        remote(r, r, sem.at[0], sem.at[2], e, left).start()
        remote(r, r, sem.at[4], sem.at[5], e, sib).start()

    def gather_rest(view, sem):
        for k, xs in ((1, xl), (2, xr), (3, xo)):
            r = view(xs)
            wait_recv(r, sem.at[k])
            remote(r, r, sem.at[4], sem.at[5], e, sib).start()

    @pl.when(c == 0)
    def _():
        up = remote(
            mgx.at[F : F + 16, :], mgx.at[0:16, :], mhsem.at[0], mhsem.at[1], after, t
        )
        down = remote(
            mgx.at[16:32, :], mgx.at[16 + F : EXT, :], mhsem.at[2], mhsem.at[3], before, t
        )
        up.start()
        down.start()
        gates_home()

        @pl.loop(0, NQ)
        def _(q):
            fgall[16 : F - 16, full_ds(x * DX + q * 128, 128)] = conv(
                mgx, x, q, True, 16, F - 32
            ).astype(BF16)

        up.wait_recv()
        down.wait_recv()
        for q in range(NQ):
            tile = full_ds(x * DX + q * 128, 128)
            for lo in (0, F - 16):
                fgall[lo : lo + 16, tile] = conv(mgx, x, q, True, lo, 16).astype(BF16)
            gather_own(fgall.at[:, tile], fgsem)
        gather_rest(lambda xs: fgall.at[:, full_ds(xs * DX, DX)], fgsem)
        for k, xs in ((0, x), (1, xl), (2, xr), (3, xo)):
            wait_recv(kfull.at[xs], kfsem.at[k])
        wait_send(fgall.at[:, 0 : 3 * DX], fgsem.at[0])
        wait_send(fgall, fgsem.at[4])
        up.wait_send()
        down.wait_send()

    @pl.when(c == 1)
    def _():
        kg[...] = jnp.zeros_like(kg)
        for j in range(NE):
            if j < KW:
                near = sx[j + 1 : j + 1 + F, :] == sx[16 : 16 + F, :]
                for q in range(NQ):
                    cols = slice(q * 128, q * 128 + 128)
                    prod = jnp.where(
                        near, fx[j + 1 : j + 1 + F, cols] * mgx[16 : 16 + F, cols], 0.0
                    )
                    kg[j, q : q + 1, :] = jnp.sum(prod, axis=0, keepdims=True)

            if j % 8 == 7:

                @pl.when(y != j // 8)
                def _():
                    remote(
                        kg.at[j - 7 : j + 1], krecv.at[y], ksem.at[0], ksem.at[1],
                        z * NY + j // 8, t,
                    ).start()

                @pl.when(y == j // 8)
                def _():
                    krecv[y] = kg[j - 7 : j + 1]

        gates_home()
        wait_recv(krecv.at[1:NY], ksem.at[1])
        kz[z] = jnp.sum(krecv[...], axis=0)
        for k in (4, 3, 5, 2, 6, 1, 7):
            remote(kz.at[z], kz.at[z], ksem.at[2], ksem.at[3], zt[k] + y, t).start()
        wait_recv(kz.at[1:NZ], ksem.at[3])
        own = pl.ds(pl.multiple_of(y * 8, 8), 8)
        kfull[x, own] = jnp.sum(kz[...], axis=0)
        mine = kfull.at[x, own]
        for k, xs in ((3, xo), (1, xr), (2, xl), (0, x)):
            for m in (2, 1, 3, 0):
                for cc in (0, 1):
                    if k == 0 and m == 0 and cc == 1:
                        continue
                    remote(
                        mine, mine, kfsem.at[4], kfsem.at[k], z * NY + yt[m], 2 * xs + cc
                    ).start()
        wait_recv(kfull.at[x, 0:24], kfsem.at[0])
        for k, xs in ((1, xl), (2, xr), (3, xo)):
            wait_recv(kfull.at[xs], kfsem.at[k])
        wait_recv(fgall, fgsem.at[5])
        wait_send(krecv.at[1:NY], ksem.at[0])
        wait_send(kz.at[1:NZ], ksem.at[2])
        wait_send(ip.at[0:496, 0:512], kfsem.at[4])

    wait_recv(gg.at[1 : 2 * NX], ggsem.at[1])
    gg_out[...] = jnp.sum(gg[...], axis=0)
    fg_out[...] = fgall[...]
    for xs in range(NX):
        for q in range(NQ):
            kg_out[:, xs * DX + q * 128 : xs * DX + q * 128 + 128] = kfull[xs, 0:KW, q, :]

    halo_up.wait_send()
    halo_down.wait_send()
    wait_send(sendbuf.at[0, CAP:SLOTS, :], asend.at[0])
    wait_send(sendbuf.at[1, CAP:SLOTS, :], asend.at[2])

    @pl.when(c == 1)
    def _():
        wait_send(grecv.at[1:NE], asend.at[1])
        share.wait_send()

    wait_send(rows.at[c, :, xcols], xsend.at[0])
    wait_send(rows.at[c, :, xcols], xsend.at[1])
    wait_send(rows.at[c], ssend.at[0])
    wait_send(gpx.at[1 : 2 * NX], gpsem.at[0])

    @pl.when(t == 0)
    def _():
        wait_send(gpret.at[1:NY], gpsem.at[2])

    @pl.when(t > 0)
    def _():
        wait_send(gpret, gpsem.at[2])

    wait_send(sibrecv, sibsem.at[0])
    wait_send(r1.at[:, 0], rsem.at[0])
    wait_send(r1.at[:, 1], rsem.at[1])
    wait_send(s2.at[:, 0], rsem.at[2])
    wait_send(s2.at[:, 1], rsem.at[3])

    @pl.when(c == 0)
    def _():
        wait_send(ip.at[CAP:SLOTS, 0:DX], retsem.at[0])

    @pl.when(c == 1)
    def _():
        wait_send(ip.at[:, 0:DX], retsem.at[0])

    wait_send(gg.at[1 : 2 * NX], ggsem.at[0])


def write_out(*refs):
    copies = [pltpu.make_async_copy(refs[k], refs[5 + k], refs[10].at[k]) for k in range(5)]
    for copy in copies:
        copy.start()
    for copy in copies:
        copy.wait()


def on_device(frames, cotangent, segment_ids, kernel, expert_ids, gates, w_in, w_out):
    vmem = pl.BlockSpec(memory_space=pltpu.VMEM)
    hbm = pl.BlockSpec(memory_space=pltpu.HBM)
    dma = pltpu.SemaphoreType.DMA
    V = pltpu.VMEM
    scratch = dict(
        frames=V((F, D), BF16),
        cot=V((F, D), BF16),
        seg=V((1, F), jnp.int32),
        kern=V((KW, D), F32),
        ids=V((2, F), jnp.int32),
        gates=V((2, F), BF16),
        win=V((D, HS), BF16),
        wout=V((HS, D), BF16),
        rows=V((2, SLOTS, D), BF16),
        sendbuf=V((2, SLOTS, DX), BF16),
        src=V((2, F, DX), BF16),
        hs=V((2, 16, 2 * DX + 128), BF16),
        hr=V((2, 16, 2 * DX + 128), BF16),
        fx=V((EXT, DX), F32),
        fx2=V((EXT, DX), F32),
        sx=V((EXT, 128), F32),
        gsend=V((4, 1, 128), F32),
        grecv=V((NE, 1, 128), F32),
        wcol=V((SLOTS, 128), F32),
        scaled=V((SLOTS, D), BF16),
        hidden=V((SLOTS, HS), BF16),
        pgrad=V((SLOTS, HS), BF16),
        gacc=V((SLOTS, 128), F32),
        gpsend=V((4, 1, 128), F32),
        gpx=V((2 * NX, 1, 128), F32),
        gprow=V((1, 1, 128), F32),
        gpret=V((NY, 1, 128), F32),
        ip=V((SLOTS, D), BF16),
        sibrecv=V((4, HF, D), BF16),
        cs=V((4, HF, D), BF16),
        r1=V((4, 2, HF // 2, DX), BF16),
        s2=V((4, 2, HF, DX), BF16),
        r2=V((4, 2, HF, DX), BF16),
        fin=V((4, HF, DX), BF16),
        ret=V((SLOTS, DX), BF16),
        mgx=V((EXT, DX), F32),
        fgall=V((F, D), BF16),
        kg=V((NE, 4, 128), F32),
        krecv=V((NY, 8, 4, 128), F32),
        kz=V((NZ, 8, 4, 128), F32),
        kfull=V((NX, NE, 4, 128), F32),
        gg=V((2 * NX, 2, 128), F32),
        posr=V((2, F, F), jnp.int32),
        posc=V((2, F, F), jnp.int32),
        lsem=dma((8,)),
        hsem=dma((4,)),
        asend=dma((3,)),
        arecv=dma((8,)),
        gsem=dma((3,)),
        xsend=dma((2,)),
        ssend=dma((1,)),
        fl=dma((4,)),
        fr=dma((4,)),
        fs=dma((4,)),
        gpsem=dma((4,)),
        sibsem=dma((9,)),
        rsem=dma((20,)),
        retsem=dma((2,)),
        mhsem=dma((4,)),
        fgsem=dma((6,)),
        ksem=dma((4,)),
        kfsem=dma((5,)),
        ggsem=dma((2,)),
    )
    made = pl.pallas_call(
        body,
        out_shape=(
            V((F, D), BF16),
            V((KW, D), F32),
            V((D, HS), BF16),
            V((HS, D), BF16),
            V((2, F), F32),
        ),
        in_specs=[hbm] * 8,
        out_specs=(vmem,) * 5,
        scratch_shapes=list(scratch.values()),
        compiler_params=pltpu.CompilerParams(
            collective_id=0, has_side_effects=True, vmem_limit_bytes=56 * 1024 * 1024
        ),
    )(
        frames,
        cotangent,
        segment_ids.reshape(1, F),
        kernel,
        expert_ids.T,
        gates.T,
        w_in[0],
        w_out[0],
    )
    fg, kg, wig, wog, gg = pl.pallas_call(
        write_out,
        out_shape=tuple(pltpu.HBM(v.shape, v.dtype) for v in made),
        in_specs=[vmem] * 5,
        out_specs=(hbm,) * 5,
        scratch_shapes=[dma((5,))],
        compiler_params=pltpu.CompilerParams(vmem_limit_bytes=2 * 1024 * 1024),
    )(*made)
    return fg, kg, wig[None], wog[None], gg.T


def solution(mesh):
    return jax.shard_map(
        on_device,
        mesh=mesh,
        in_specs=(
            P("expert", None),
            P("expert", None),
            P("expert"),
            P(),
            P("expert", None),
            P("expert", None),
            P("expert", None, "tensor"),
            P("expert", "tensor", None),
        ),
        out_specs=(
            P("expert", None),
            P(),
            P("expert", None, "tensor"),
            P("expert", "tensor", None),
            P("expert", None),
        ),
        check_vma=False,
    )
```

```python
import jax
import jax.numpy as jnp
from jax import lax
from jax.experimental import pallas as pl
from jax.experimental.pallas import tpu as pltpu
from jax.sharding import PartitionSpec as P

MESH = pl.DeviceIdType.MESH
F32 = jnp.float32
BF16 = jnp.bfloat16
NZ, NY, NX = 8, 4, 4
NE = NZ * NY
F = 128
HF = F // 2
D = 1536
HS = 768
KW = 31
CAP = 16
SLOTS = NE * CAP
DX = D // NX
NQ = DX // 128
EXT = F + 32


def full_ds(start, size):
    return pl.ds(pl.multiple_of(start, 128), size)


def body(
    frames_in, cot_in, seg_in, kern_in, ids_in, gates_in, w_in, w_out,
    fg_out, kg_out, wig, wog, gg_out,
    frames, cot, seg, kern, ids, gates,
    win, wout, rows, sendbuf, src, hs, hr, fx, fx2, sx, gsend, grecv, wcol,
    scaled, hidden, pgrad, gacc, gpsend, gpx, gprow, gpret, ip, sibrecv, cs, r1, s2, r2, fin, ret,
    mgx, fgall, kg, krecv, kz, kfull, gg, posr, posc,
    lsem, hsem, asend, arecv, gsem, xsend, ssend, fl, fr, fs, gpsem, sibsem, rsem,
    retsem, mhsem, fgsem, ksem, kfsem, ggsem,
):
    e = lax.axis_index("expert")
    t = lax.axis_index("tensor")
    z, y = lax.div(e, NY), lax.rem(e, NY)
    x, c = lax.div(t, 2), lax.rem(t, 2)
    sib = t + 1 - 2 * c
    xr, xl, xo = lax.rem(x + 1, NX), lax.rem(x + 3, NX), lax.rem(x + 2, NX)
    right, left, facing = xr * 2 + c, xl * 2 + c, xo * 2 + c
    xcols = full_ds(x * DX, DX)

    zt = [lax.rem(z + k, NZ) * NY for k in range(NZ)]
    yt = [lax.rem(y + k, NY) for k in range(NY)]

    def offset(i):
        p = i // NY
        return ((p + 1) // 2 if p % 2 else (NZ - p // 2) % NZ), i % NY

    def ahead(i):
        dz, dy = offset(i)
        return zt[dz] + yt[dy]

    def behind(i):
        dz, dy = offset(i)
        return zt[(NZ - dz) % NZ] + yt[(NY - dy) % NY]

    def remote(s, d, ss, rs, ee, tt):
        return pltpu.make_async_remote_copy(
            src_ref=s, dst_ref=d, send_sem=ss, recv_sem=rs, device_id=(ee, tt), device_id_type=MESH
        )

    def wait_recv(ref, sem):
        remote(ref, ref, sem, sem, e, sib).wait_recv()

    def wait_send(ref, sem):
        remote(ref, ref, sem, sem, e, sib).wait_send()

    barrier = pltpu.get_barrier_semaphore()

    for i in range(1, NE):
        for tt in (t, sib):
            pl.semaphore_signal(barrier, inc=1, device_id=(ahead(i), tt), device_id_type=MESH)
    for i in range(1, 2 * NX):
        pl.semaphore_signal(
            barrier, inc=1, device_id=(e, lax.rem(t + i, 2 * NX)), device_id_type=MESH
        )
    for tt in (right, left, facing, right + sib - t, left + sib - t, facing + sib - t):
        for m in range(1, NY):
            pl.semaphore_signal(
                barrier, inc=1, device_id=(z * NY + yt[m], tt), device_id_type=MESH
            )
    pairs = (
        (ids_in, ids), (gates_in, gates), (seg_in, seg), (frames_in, frames), (cot_in, cot),
        (kern_in, kern), (w_in, win), (w_out, wout),
    )
    loads = [pltpu.make_async_copy(a, b, lsem.at[k]) for k, (a, b) in enumerate(pairs)]
    for load in loads:
        load.start()
    for load in loads[:3]:
        load.wait()

    lane = lax.broadcasted_iota(jnp.int32, (F, F), 1)
    sub = lax.broadcasted_iota(jnp.int32, (F, F), 0)
    eye = lane == sub
    idr = [jnp.broadcast_to(ids[k : k + 1, :], (F, F)).astype(F32) for k in range(2)]
    idc = [v.T for v in idr]

    def place(idf, rank):
        idv = idf.astype(jnp.int32)
        dz = (idv // NY - z + NZ) & (NZ - 1)
        dy = (idv - (idv // NY) * NY - y + NY) & (NY - 1)
        p = jnp.maximum(jnp.where(dz <= NZ // 2, 2 * dz - 1, 2 * NZ - 2 * dz), 0)
        return (p * NY + dy) * CAP + rank.astype(jnp.int32)

    for k in range(2):
        hits = jnp.where(idc[0] == idr[k], 1.0, 0.0) + jnp.where(idc[1] == idr[k], 1.0, 0.0)
        rank = jnp.sum(jnp.where(sub < lane, hits, 0.0), axis=0, keepdims=True)
        posr[k] = place(idr[k], jnp.broadcast_to(rank, (F, F)))
        hits = jnp.where(idr[0] == idc[k], 1.0, 0.0) + jnp.where(idr[1] == idc[k], 1.0, 0.0)
        rank = jnp.sum(jnp.where(lane < sub, hits, 0.0), axis=1, keepdims=True)
        posc[k] = place(idc[k], jnp.broadcast_to(rank, (F, F)))

    for g in range(4):
        total = jnp.zeros((1, F), F32)
        for k in range(2):
            gcol = jnp.broadcast_to(gates[k : k + 1, :].astype(F32), (F, F)).T
            total += jnp.sum(
                jnp.where(posc[k] == lane + g * F, gcol, 0.0), axis=0, keepdims=True
            )
        gsend[g] = total

    @pl.when(c == 1)
    def _():
        grecv[0] = gsend[0]

    for load in loads[3:6]:
        load.wait()
    segr = jnp.broadcast_to(seg[...], (F, F)).astype(F32)
    segc = segr.T
    sx[16 : 16 + F, :] = segc
    ocols = full_ds(xo * DX, DX)
    for k, rs in enumerate((slice(0, 16), slice(F - 16, F))):
        hs[k, :, 0:DX] = frames[rs, xcols]
        hs[k, :, DX : 2 * DX] = frames[rs, ocols]
        hs[k, :, 2 * DX : 2 * DX + 128] = segc[rs].astype(BF16)

    @pl.loop(0, NQ)
    def _(q):
        tile = full_ds(q * 128, 128)
        fx[16 : 16 + F, tile] = frames[:, full_ds(x * DX + q * 128, 128)].astype(F32)
        fx2[16 : 16 + F, tile] = frames[:, full_ds(xo * DX + q * 128, 128)].astype(F32)

    def conv(ext, xs, q, backwards, lo, n):
        cols = full_ds(q * 128, 128)
        kcols = full_ds(xs * DX + q * 128, 128)
        acc = ext[16 + lo : 16 + lo + n, cols]
        own = sx[16 + lo : 16 + lo + n, :]
        for j in range(KW):
            tap = kern[KW - 1 - j if backwards else j, kcols].reshape(1, 128)
            near = slice(j + 1 + lo, j + 1 + lo + n)
            acc += jnp.where(sx[near, :] == own, ext[near, cols] * tap, 0.0)
        return acc

    @pl.when(c == 0)
    def _():
        for part, (ext, xs) in enumerate(((fx, x), (fx2, xo))):

            @pl.loop(0, NQ)
            def _(q):
                src[part, 16 : F - 16, full_ds(q * 128, 128)] = conv(
                    ext, xs, q, False, 16, F - 32
                ).astype(BF16)

    @pl.when(c == 1)
    def _():
        src[0] = cot[:, xcols]
        src[1] = cot[:, ocols]

    pl.semaphore_wait(barrier, 2 * (NE - 1) + 2 * NX - 1 + 6 * (NY - 1))

    before, after = lax.rem(e + NE - 1, NE), lax.rem(e + 1, NE)
    halo_up = remote(hs.at[1], hr.at[0], hsem.at[0], hsem.at[1], after, t)
    halo_down = remote(hs.at[0], hr.at[1], hsem.at[2], hsem.at[3], before, t)
    halo_up.start()
    halo_down.start()

    def take_halo():
        halo_up.wait_recv()
        halo_down.wait_recv()
        for k, rs in enumerate((slice(0, 16), slice(16 + F, EXT))):
            fx[rs, :] = hr[k, :, 0:DX].astype(F32)
            fx2[rs, :] = hr[k, :, DX : 2 * DX].astype(F32)
        sx[0:16, :] = jnp.where(e == 0, -1.0, hr[0, :, 2 * DX : 2 * DX + 128].astype(F32))
        sx[16 + F : EXT, :] = jnp.where(
            e == NE - 1, -1.0, hr[1, :, 2 * DX : 2 * DX + 128].astype(F32)
        )

    def source(part, ext, xs):
        @pl.when(c == 0)
        def _():
            if part == 0:
                take_halo()

            @pl.loop(0, NQ)
            def _(q):
                cols = full_ds(q * 128, 128)
                for lo in (0, F - 16):
                    src[part, lo : lo + 16, cols] = conv(ext, xs, q, False, lo, 16).astype(BF16)

    def issue(part, xs, g):
        cols = full_ds(xs * DX, DX)
        slot = sub + g * F
        onehot = jnp.where((posr[0] == slot) | (posr[1] == slot), 1.0, 0.0).astype(BF16)
        sendbuf[part, g * F : g * F + F, :] = jnp.dot(
            onehot, src[part], preferred_element_type=F32
        ).astype(BF16)
        for i in range(max(8 * g, 1), 8 * g + 8):
            blk = slice(i * CAP, i * CAP + CAP)
            remote(
                sendbuf.at[part, blk, :], rows.at[c, blk, cols], asend.at[2 * part],
                arecv.at[4 * part + g], ahead(i), t,
            ).start()
        if g == 0:
            rows[c, 0:CAP, cols] = sendbuf[part, 0:CAP, :]

    source(0, fx, x)
    for g in range(4):
        issue(0, x, g)
    @pl.when(c == 1)
    def _():
        take_halo()

    def region(g, xs):
        return rows.at[c, g * F : g * F + F, full_ds(xs * DX, DX)]

    def to_sibling(g, xs):
        r = region(g, xs)
        remote(r, r, ssend.at[0], fs.at[g], e, sib).start()

    def arrive(part, xs, g):
        if g == 0:
            wait_recv(rows.at[c, CAP:F, full_ds(xs * DX, DX)], arecv.at[4 * part])
        else:
            wait_recv(region(g, xs), arecv.at[4 * part + g])

    def spread(g):
        arrive(0, x, g)
        r = region(g, x)
        remote(r, r, xsend.at[0], fl.at[g], e, right).start()
        remote(r, r, xsend.at[1], fr.at[g], e, left).start()
        to_sibling(g, x)

    def relay(g):
        wait_recv(region(g, xl), fl.at[g])
        to_sibling(g, xl)
        wait_recv(region(g, xr), fr.at[g])
        to_sibling(g, xr)

    def opposite(g):
        arrive(1, xo, g)
        to_sibling(g, xo)

    def from_sibling(g):
        wait_recv(rows.at[1 - c, g * F : g * F + F, :], fs.at[g])

    def weigh(g):
        parts = [jnp.broadcast_to(grecv[8 * g + q], (CAP, F)) for q in range(8)]
        w = jnp.sum(jnp.where(eye, jnp.concatenate(parts, axis=0), 0.0), axis=1, keepdims=True)
        wcol[g * F : g * F + F, :] = jnp.broadcast_to(w, (F, 128))

    def work(h):
        hr_ = slice(256 * h, 256 * h + 256)
        gacc[hr_, :] = jnp.zeros((256, 128), F32)

        @pl.loop(0, HS // 768)
        def _(n):
            cols = full_ds(n * 768, 768)
            pre = jnp.dot(rows[0, hr_, :], win[:, cols], preferred_element_type=F32)
            back = lax.dot_general(
                rows[1, hr_, :], wout[cols, :], (((1,), (1,)), ((), ())), preferred_element_type=F32
            )
            sig = jax.nn.sigmoid(pre)
            hid = (pre * sig).astype(BF16)
            hidden[hr_, cols] = hid
            prod = hid.astype(F32) * back
            for m in range(0, 768, 128):
                gacc[hr_, :] += prod[:, m : m + 128]
            w = wcol[hr_, 0:1]
            pgrad[hr_, cols] = (back * w * (sig * (1.0 + pre * (1.0 - sig)))).astype(BF16)

        for g in (2 * h, 2 * h + 1):
            part = jnp.sum(gacc[g * F : g * F + F, :], axis=1, keepdims=True)
            gpsend[g] = jnp.sum(
                jnp.where(eye, jnp.broadcast_to(part, (F, F)), 0.0), axis=0, keepdims=True
            )

        for tt in range(4 * h, 4 * h + 4):

            @pl.when(t == tt)
            def _():
                gpx[tt] = gpsend[tt // 2]

            @pl.when(t != tt)
            def _():
                remote(
                    gpsend.at[tt // 2], gpx.at[t], gpsem.at[0], gpsem.at[1], e, tt
                ).start()

    def gates_on():
        wait_recv(gpx.at[1 : 2 * NX], gpsem.at[1])
        gprow[0] = jnp.sum(gpx[...], axis=0)
        dz = c * (x + 1) + (1 - c) * lax.rem(NZ - x, NZ)
        zz = lax.rem(z + NZ - dz, NZ) * NY

        @pl.when(t == 0)
        def _():
            gpret[0] = gprow[0]

        @pl.when(t > 0)
        def _():
            remote(gprow.at[0], gpret.at[0], gpsem.at[2], gpsem.at[3], zz + yt[0], t).start()

        for j in range(1, NY):
            remote(
                gprow.at[0], gpret.at[j], gpsem.at[2], gpsem.at[3], zz + yt[NY - j], t
            ).start()

    def gates_home():
        @pl.when(t == 0)
        def _():
            wait_recv(gpret.at[1:NY], gpsem.at[3])

        @pl.when(t > 0)
        def _():
            wait_recv(gpret, gpsem.at[3])

        row = jnp.zeros((1, F), F32)
        for j in range(NY):
            row += jnp.where(lax.div(lane[0:1, :], CAP) == 4 * c + j, gpret[j], 0.0)
        row = jnp.broadcast_to(row, (F, F))
        for k in range(2):
            hit = jnp.where(posc[k] == lane + x * F, row, 0.0)
            col = jnp.sum(hit, axis=1, keepdims=True)
            gg[t, k : k + 1, :] = jnp.sum(
                jnp.where(eye, jnp.broadcast_to(col, (F, F)), 0.0), axis=0, keepdims=True
            )
        for i in range(1, 2 * NX):
            remote(
                gg.at[t], gg.at[t], ggsem.at[0], ggsem.at[1], e, lax.rem(t + i, 2 * NX)
            ).start()

    def scale():
        @pl.loop(0, D // 256)
        def _(n):
            cols = full_ds(n * 256, 256)
            for h in range(4):
                rh = slice(F * h, F * h + F)
                scaled[rh, cols] = (wcol[rh, 0:1] * rows[1, rh, cols].astype(F32)).astype(BF16)

    def inputs_grad(h):
        rh = slice(256 * h, 256 * h + 256)

        for k, xs in enumerate((xo, xr, xl, x)):
            cols = full_ds(xs * DX, DX)
            ip[rh, cols] = lax.dot_general(
                pgrad[rh, :], win[cols, :], (((1,), (1,)), ((), ())), preferred_element_type=F32
            ).astype(BF16)
            for g in (2 * h, 2 * h + 1):
                other = pl.ds(pl.multiple_of(F * g + (1 - c) * HF, HF), HF)
                arrived = sibsem.at[(1 if k == 0 else 5) + g]
                remote(
                    ip.at[other, cols], sibrecv.at[g, :, cols], sibsem.at[0], arrived, e, sib
                ).start()

    def ring1(h):
        oc = full_ds(xo * DX, DX)
        wait_recv(sibrecv.at[h, :, oc], sibsem.at[1 + h])
        own = pl.ds(pl.multiple_of(F * h + c * HF, HF), HF)
        cs[h, :, oc] = (ip[own, oc].astype(F32) + sibrecv[h, :, oc].astype(F32)).astype(BF16)
        remote(cs.at[h, 0:32, oc], r1.at[h, 0], rsem.at[0], rsem.at[4 + h], e, right).start()
        remote(cs.at[h, 32:64, oc], r1.at[h, 1], rsem.at[1], rsem.at[8 + h], e, left).start()

        wait_recv(sibrecv.at[h, :, 0 : 3 * DX], sibsem.at[5 + h])
        for xs in (xr, xl, x):
            cols = full_ds(xs * DX, DX)
            cs[h, :, cols] = (
                ip[own, cols].astype(F32) + sibrecv[h, :, cols].astype(F32)
            ).astype(BF16)

    def ring2(h):
        wait_recv(r1.at[h, 0], rsem.at[4 + h])
        rc = full_ds(xr * DX, DX)
        s2[h, 0, 0:32, :] = (cs[h, 0:32, rc].astype(F32) + r1[h, 0].astype(F32)).astype(BF16)
        s2[h, 0, 32:64, :] = cs[h, 32:64, rc]
        remote(s2.at[h, 0], r2.at[h, 0], rsem.at[2], rsem.at[12 + h], e, right).start()
        wait_recv(r1.at[h, 1], rsem.at[8 + h])
        lc = full_ds(xl * DX, DX)
        s2[h, 1, 32:64, :] = (cs[h, 32:64, lc].astype(F32) + r1[h, 1].astype(F32)).astype(BF16)
        s2[h, 1, 0:32, :] = cs[h, 0:32, lc]
        remote(s2.at[h, 1], r2.at[h, 1], rsem.at[3], rsem.at[16 + h], e, left).start()

    def ring3(h):
        wait_recv(r2.at[h, 0], rsem.at[12 + h])
        wait_recv(r2.at[h, 1], rsem.at[16 + h])
        fin[h] = (
            cs[h, :, xcols].astype(F32) + r2[h, 0].astype(F32) + r2[h, 1].astype(F32)
        ).astype(BF16)

        for q in range(4):
            blk = slice(q * CAP, q * CAP + CAP)
            i = 8 * h + q

            def send():
                to = jnp.where(c == 0, behind(i), behind(i + 4))
                place = pl.ds(pl.multiple_of(i * CAP + c * HF, CAP), CAP)
                for tt in (t, sib):
                    remote(
                        fin.at[h, blk, :], ret.at[place, :], retsem.at[0], retsem.at[1], to, tt
                    ).start()

            if i == 0:

                @pl.when(c == 0)
                def _():
                    ret[0:CAP, :] = fin[0, 0:CAP, :]
                    remote(
                        fin.at[h, blk, :], ret.at[0:CAP, :], retsem.at[0], retsem.at[1], e, sib
                    ).start()

                pl.when(c == 1)(send)
            else:
                send()

    def first_grad(lo, hi):
        @pl.loop(lo, hi)
        def _(m):
            cols = full_ds(m * 256, 256)
            wig[cols, :] = lax.dot_general(
                rows[0, :, cols], pgrad[...], (((0,), (0,)), ((), ())), preferred_element_type=F32
            ).astype(BF16)

    def second_grad(lo, hi):
        @pl.loop(lo, hi)
        def _(m):
            cols = full_ds(m * 256, 256)
            for n in range(2):
                nc = slice(n * 768, n * 768 + 768)
                wog[cols, nc] = lax.dot_general(
                    hidden[:, cols], scaled[:, nc], (((0,), (0,)), ((), ())),
                    preferred_element_type=F32,
                ).astype(BF16)

    source(1, fx2, xo)
    issue(1, xo, 0)
    issue(1, xo, 1)
    spread(0)
    issue(1, xo, 2)
    issue(1, xo, 3)
    spread(1)

    @pl.when(c == 1)
    def _():
        for i in range(1, NE):
            remote(
                gsend.at[i // 8], grecv.at[i], asend.at[1], gsem.at[0], ahead(i), t
            ).start()

    spread(2)
    spread(3)
    opposite(0)
    relay(0)
    opposite(1)

    share = remote(grecv, grecv, gsem.at[1], gsem.at[2], e, sib)

    @pl.when(c == 1)
    def _():
        wait_recv(grecv.at[1:NE], gsem.at[0])
        share.start()

    relay(1)

    @pl.when(c == 0)
    def _():
        share.wait_recv()

    for g in range(4):
        weigh(g)
    for load in loads[6:]:
        load.wait()
    from_sibling(0)
    from_sibling(1)
    work(0)
    opposite(2)
    relay(2)
    opposite(3)
    relay(3)
    inputs_grad(0)
    from_sibling(2)
    from_sibling(3)
    ring1(0)
    ring1(1)
    work(1)
    ring2(0)
    ring2(1)
    inputs_grad(1)
    ring1(2)
    ring1(3)
    ring3(0)
    ring3(1)
    ring2(2)
    ring2(3)
    gates_on()
    first_grad(0, 2)
    ring3(2)
    ring3(3)
    first_grad(2, 6)
    scale()
    second_grad(0, 3)

    @pl.when(c == 0)
    def _():
        wait_recv(ret.at[CAP:SLOTS, :], retsem.at[1])

    @pl.when(c == 1)
    def _():
        wait_recv(ret, retsem.at[1])

    mg = cot[:, xcols].astype(F32)
    for g in range(4):
        slot = lane + g * F
        pick = jnp.where((posc[0] == slot) | (posc[1] == slot), 1.0, 0.0).astype(BF16)
        mg += jnp.dot(pick, ret[g * F : g * F + F, :], preferred_element_type=F32)
    mgx[16 : 16 + F, :] = mg

    def gather_own(r, sem):
        remote(r, r, sem.at[0], sem.at[3], e, facing).start()
        remote(r, r, sem.at[0], sem.at[1], e, right).start()
        remote(r, r, sem.at[0], sem.at[2], e, left).start()
        remote(r, r, sem.at[4], sem.at[5], e, sib).start()

    def gather_rest(view, sem):
        for k, xs in ((1, xl), (2, xr), (3, xo)):
            r = view(xs)
            wait_recv(r, sem.at[k])
            remote(r, r, sem.at[4], sem.at[5], e, sib).start()

    @pl.when(c == 0)
    def _():
        up = remote(
            mgx.at[F : F + 16, :], mgx.at[0:16, :], mhsem.at[0], mhsem.at[1], after, t
        )
        down = remote(
            mgx.at[16:32, :], mgx.at[16 + F : EXT, :], mhsem.at[2], mhsem.at[3], before, t
        )
        up.start()
        down.start()
        gates_home()

        @pl.loop(0, NQ)
        def _(q):
            fgall[16 : F - 16, full_ds(x * DX + q * 128, 128)] = conv(
                mgx, x, q, True, 16, F - 32
            ).astype(BF16)

        up.wait_recv()
        down.wait_recv()
        for q in range(NQ):
            tile = full_ds(x * DX + q * 128, 128)
            for lo in (0, F - 16):
                fgall[lo : lo + 16, tile] = conv(mgx, x, q, True, lo, 16).astype(BF16)
            gather_own(fgall.at[:, tile], fgsem)
        gather_rest(lambda xs: fgall.at[:, full_ds(xs * DX, DX)], fgsem)
        for k, xs in ((0, x), (1, xl), (2, xr), (3, xo)):
            wait_recv(kfull.at[xs], kfsem.at[k])
        wait_send(fgall.at[:, 0 : 3 * DX], fgsem.at[0])
        wait_send(fgall, fgsem.at[4])
        up.wait_send()
        down.wait_send()

    @pl.when(c == 1)
    def _():
        kg[...] = jnp.zeros_like(kg)
        for j in range(NE):
            if j < KW:
                near = sx[j + 1 : j + 1 + F, :] == sx[16 : 16 + F, :]
                for q in range(NQ):
                    cols = slice(q * 128, q * 128 + 128)
                    prod = jnp.where(
                        near, fx[j + 1 : j + 1 + F, cols] * mgx[16 : 16 + F, cols], 0.0
                    )
                    kg[j, q : q + 1, :] = jnp.sum(prod, axis=0, keepdims=True)

            if j % 8 == 7:

                @pl.when(y != j // 8)
                def _():
                    remote(
                        kg.at[j - 7 : j + 1], krecv.at[y], ksem.at[0], ksem.at[1],
                        z * NY + j // 8, t,
                    ).start()

                @pl.when(y == j // 8)
                def _():
                    krecv[y] = kg[j - 7 : j + 1]

        gates_home()
        wait_recv(krecv.at[1:NY], ksem.at[1])
        kz[z] = jnp.sum(krecv[...], axis=0)
        for k in (4, 3, 5, 2, 6, 1, 7):
            remote(kz.at[z], kz.at[z], ksem.at[2], ksem.at[3], zt[k] + y, t).start()
        wait_recv(kz.at[1:NZ], ksem.at[3])
        own = pl.ds(pl.multiple_of(y * 8, 8), 8)
        kfull[x, own] = jnp.sum(kz[...], axis=0)
        mine = kfull.at[x, own]
        for k, xs in ((3, xo), (1, xr), (2, xl), (0, x)):
            for m in (2, 1, 3, 0):
                for cc in (0, 1):
                    if k == 0 and m == 0 and cc == 1:
                        continue
                    remote(
                        mine, mine, kfsem.at[4], kfsem.at[k], z * NY + yt[m], 2 * xs + cc
                    ).start()
        wait_recv(kfull.at[x, 0:24], kfsem.at[0])
        for k, xs in ((1, xl), (2, xr), (3, xo)):
            wait_recv(kfull.at[xs], kfsem.at[k])
        wait_recv(fgall, fgsem.at[5])
        wait_send(krecv.at[1:NY], ksem.at[0])
        wait_send(kz.at[1:NZ], ksem.at[2])
        wait_send(ip.at[0:496, 0:512], kfsem.at[4])

    wait_recv(gg.at[1 : 2 * NX], ggsem.at[1])
    gg_out[...] = jnp.sum(gg[...], axis=0)
    fg_out[...] = fgall[...]
    for xs in range(NX):
        for q in range(NQ):
            kg_out[:, xs * DX + q * 128 : xs * DX + q * 128 + 128] = kfull[xs, 0:KW, q, :]

    halo_up.wait_send()
    halo_down.wait_send()
    wait_send(sendbuf.at[0, CAP:SLOTS, :], asend.at[0])
    wait_send(sendbuf.at[1, CAP:SLOTS, :], asend.at[2])

    @pl.when(c == 1)
    def _():
        wait_send(grecv.at[1:NE], asend.at[1])
        share.wait_send()

    wait_send(rows.at[c, :, xcols], xsend.at[0])
    wait_send(rows.at[c, :, xcols], xsend.at[1])
    wait_send(rows.at[c], ssend.at[0])
    wait_send(gpx.at[1 : 2 * NX], gpsem.at[0])

    @pl.when(t == 0)
    def _():
        wait_send(gpret.at[1:NY], gpsem.at[2])

    @pl.when(t > 0)
    def _():
        wait_send(gpret, gpsem.at[2])

    wait_send(sibrecv, sibsem.at[0])
    wait_send(r1.at[:, 0], rsem.at[0])
    wait_send(r1.at[:, 1], rsem.at[1])
    wait_send(s2.at[:, 0], rsem.at[2])
    wait_send(s2.at[:, 1], rsem.at[3])

    @pl.when(c == 0)
    def _():
        wait_send(ip.at[CAP:SLOTS, 0:DX], retsem.at[0])

    @pl.when(c == 1)
    def _():
        wait_send(ip.at[:, 0:DX], retsem.at[0])

    wait_send(gg.at[1 : 2 * NX], ggsem.at[0])


def write_out(*refs):
    copies = [pltpu.make_async_copy(refs[k], refs[5 + k], refs[10].at[k]) for k in range(5)]
    for copy in copies:
        copy.start()
    for copy in copies:
        copy.wait()


def on_device(frames, cotangent, segment_ids, kernel, expert_ids, gates, w_in, w_out):
    vmem = pl.BlockSpec(memory_space=pltpu.VMEM)
    hbm = pl.BlockSpec(memory_space=pltpu.HBM)
    dma = pltpu.SemaphoreType.DMA
    V = pltpu.VMEM
    scratch = dict(
        frames=V((F, D), BF16),
        cot=V((F, D), BF16),
        seg=V((1, F), jnp.int32),
        kern=V((KW, D), F32),
        ids=V((2, F), jnp.int32),
        gates=V((2, F), BF16),
        win=V((D, HS), BF16),
        wout=V((HS, D), BF16),
        rows=V((2, SLOTS, D), BF16),
        sendbuf=V((2, SLOTS, DX), BF16),
        src=V((2, F, DX), BF16),
        hs=V((2, 16, 2 * DX + 128), BF16),
        hr=V((2, 16, 2 * DX + 128), BF16),
        fx=V((EXT, DX), F32),
        fx2=V((EXT, DX), F32),
        sx=V((EXT, 128), F32),
        gsend=V((4, 1, 128), F32),
        grecv=V((NE, 1, 128), F32),
        wcol=V((SLOTS, 128), F32),
        scaled=V((SLOTS, D), BF16),
        hidden=V((SLOTS, HS), BF16),
        pgrad=V((SLOTS, HS), BF16),
        gacc=V((SLOTS, 128), F32),
        gpsend=V((4, 1, 128), F32),
        gpx=V((2 * NX, 1, 128), F32),
        gprow=V((1, 1, 128), F32),
        gpret=V((NY, 1, 128), F32),
        ip=V((SLOTS, D), BF16),
        sibrecv=V((4, HF, D), BF16),
        cs=V((4, HF, D), BF16),
        r1=V((4, 2, HF // 2, DX), BF16),
        s2=V((4, 2, HF, DX), BF16),
        r2=V((4, 2, HF, DX), BF16),
        fin=V((4, HF, DX), BF16),
        ret=V((SLOTS, DX), BF16),
        mgx=V((EXT, DX), F32),
        fgall=V((F, D), BF16),
        kg=V((NE, 4, 128), F32),
        krecv=V((NY, 8, 4, 128), F32),
        kz=V((NZ, 8, 4, 128), F32),
        kfull=V((NX, NE, 4, 128), F32),
        gg=V((2 * NX, 2, 128), F32),
        posr=V((2, F, F), jnp.int32),
        posc=V((2, F, F), jnp.int32),
        lsem=dma((8,)),
        hsem=dma((4,)),
        asend=dma((3,)),
        arecv=dma((8,)),
        gsem=dma((3,)),
        xsend=dma((2,)),
        ssend=dma((1,)),
        fl=dma((4,)),
        fr=dma((4,)),
        fs=dma((4,)),
        gpsem=dma((4,)),
        sibsem=dma((9,)),
        rsem=dma((20,)),
        retsem=dma((2,)),
        mhsem=dma((4,)),
        fgsem=dma((6,)),
        ksem=dma((4,)),
        kfsem=dma((5,)),
        ggsem=dma((2,)),
    )
    made = pl.pallas_call(
        body,
        out_shape=(
            V((F, D), BF16),
            V((KW, D), F32),
            V((D, HS), BF16),
            V((HS, D), BF16),
            V((2, F), F32),
        ),
        in_specs=[hbm] * 8,
        out_specs=(vmem,) * 5,
        scratch_shapes=list(scratch.values()),
        compiler_params=pltpu.CompilerParams(
            collective_id=0, has_side_effects=True, vmem_limit_bytes=56 * 1024 * 1024
        ),
    )(
        frames,
        cotangent,
        segment_ids.reshape(1, F),
        kernel,
        expert_ids.T,
        gates.T,
        w_in[0],
        w_out[0],
    )
    fg, kg, wig, wog, gg = pl.pallas_call(
        write_out,
        out_shape=tuple(pltpu.HBM(v.shape, v.dtype) for v in made),
        in_specs=[vmem] * 5,
        out_specs=(hbm,) * 5,
        scratch_shapes=[dma((5,))],
        compiler_params=pltpu.CompilerParams(vmem_limit_bytes=2 * 1024 * 1024),
    )(*made)
    return fg, kg, wig[None], wog[None], gg.T


def solution(mesh):
    return jax.shard_map(
        on_device,
        mesh=mesh,
        in_specs=(
            P("expert", None),
            P("expert", None),
            P("expert"),
            P(),
            P("expert", None),
            P("expert", None),
            P("expert", None, "tensor"),
            P("expert", "tensor", None),
        ),
        out_specs=(
            P("expert", None),
            P(),
            P("expert", None, "tensor"),
            P("expert", "tensor", None),
            P("expert", None),
        ),
        check_vma=False,
    )
```
